32 devices in a mesh: group: 2 (over y), phi: 4 (over z), row: 2 (over core), gz: 2 (over x).
Axes of the slice: x: 2, y: 2, z: 4, core: 2. Of those that a mesh axis runs over, the one named last changes fastest.
Arguments:
- source_field: float32 [3, 128, 32, 256], P(None, ('group', 'phi'), 'gz', 'row'), parts along dimension 1, may hold values from -6 to 6
- labels: int32 [128, 32, 256], P(('group', 'phi'), 'gz', 'row'), parts along dimension 0, may hold values from 0 to 2
Outputs:
- potential: float32 [128, 32, 256], P(('group', 'phi'), 'gz', 'row'), parts along dimension 0
The draws below stay inside these ranges and needn't reach their ends.
There are 2 independent parts, one for each index of `group`. The reference program is written for one: setup_inputs(seed, part) draws one part's arguments, and reference() takes and returns one part's arrays. A program takes and returns all parts, laid end to end along the dimension named above; each array names one. Nothing has to cross between parts.
Inputs may be any that keep to these rules, and one draw needn't show every extreme that they name: `labels`: 0 is air, 1 iron, 2 coil pack.
All inputs are finite; a program needn't handle non-finite values.
Results may differ from the reference program's by a relative error of at most 0.0001.
Values sent between devices are 32-bit elements; how exact they have to be, the bound alone decides.
A program may use at most 64 MiB of HBM per device.

```python
import jax
import jax.numpy as jnp

ITERS = 4
NPHI = 64
NZ = 32
NR = 256


def touch_ends(array, stream_key, least, high):
    shape = array.shape
    spot = [jax.random.randint(jax.random.fold_in(stream_key, axis), (), 0, shape[axis]) for axis in range(len(shape))]
    array = array.at[tuple(spot)].set(least)
    longest = shape.index(max(shape))
    spot[longest] = (spot[longest] + 1) % shape[longest]
    return array.at[tuple(spot)].set(high)


def levels(rng, extent, pieces, least, largest):
    gain = 1.0
    for dim, parts in pieces:
        heights = jax.random.uniform(jax.random.fold_in(jax.random.fold_in(rng, 6), dim), (parts,), jnp.float32, least / len(pieces), largest / len(pieces))
        gain = gain * jnp.repeat(jnp.exp(heights), extent[dim] // parts).reshape((-1,) + (1,) * (len(extent) - 1 - dim))
    return gain


def scatter_about(key, dims, scale, limit, split=(), held_as=jnp.bfloat16):
    entries = scale * jax.random.normal(key, dims, jnp.float32)
    if split:
        entries = entries * levels(key, dims, split, -0.22, 0.18)
    return jnp.clip(entries, -limit, limit).astype(held_as)


def setup_inputs(seed: int = 0, part: int = 0) -> dict:
    key_list = jax.random.split(jax.random.key(seed), 3)
    part_splits = jax.random.split(jax.random.fold_in(key_list[2], part), 3)
    source_field = scatter_about(part_splits[0], (3, NPHI, NZ, NR), 1.0, 6.0, ((1, 4), (2, 2), (3, 2)), jnp.float32)
    labels = touch_ends(jax.random.randint(part_splits[1], (NPHI, NZ, NR), 0, 3), jax.random.fold_in(part_splits[1], 1), 0, 2).astype(jnp.int32)
    return {"source_field": source_field, "labels": labels}


iron_perm = 40.0
iron_sat = 0.25
coil_perm = 4.0
coil_sat = 1.0
step_cap = 0.1
spectral = 0.9

def chebyshev_weights(sweep_count):
    weights = [1.0]
    if sweep_count > 1:
        weights.append(1.0 / (1.0 - spectral * spectral / 2.0))
    while len(weights) < sweep_count:
        weights.append(1.0 / (1.0 - spectral * spectral * weights[-1] / 4.0))
    return weights

def pad_grid(values):
    leading = values.ndim - 3
    wrapped = jnp.concatenate([values[..., -1:, :, :], values, values[..., :1, :, :]], axis=leading)
    widths = [(0, 0)] * leading + [(0, 0), (1, 1), (1, 1)]
    return jnp.pad(wrapped, widths)

def neighbor(values, axis_dim, offset):
    leading = values.ndim - 3
    picks = [slice(None)] * leading
    for position in range(3):
        begin = 1 + (offset if position == axis_dim else 0)
        length = values.shape[leading + position] - 2
        picks.append(slice(begin, begin + length))
    return values[tuple(picks)]

def field_terms(padded, source_field, labels):
    field_sq = jnp.zeros(labels.shape, jnp.float32)
    for axis_dim in range(3):
        gradient = 0.5 * (neighbor(padded, axis_dim, 1) - neighbor(padded, axis_dim, -1))
        total_field = source_field[axis_dim] - gradient
        field_sq = field_sq + total_field * total_field
    iron_value = 1.0 + (iron_perm - 1.0) / (1.0 + field_sq / iron_sat)
    coil_value = 1.0 + (coil_perm - 1.0) / (1.0 + field_sq / coil_sat)
    perm = jnp.where(labels == 1, iron_value, jnp.where(labels == 2, coil_value, 1.0))
    return jnp.concatenate([(perm - 1.0)[None], perm[None] * source_field], axis=0)

def relax(padded, field_pad):
    perm_pad = 1.0 + field_pad[0]
    perm_here = neighbor(perm_pad, 0, 0)
    numerator = jnp.zeros(perm_here.shape, jnp.float32)
    denominator = jnp.zeros(perm_here.shape, jnp.float32)
    for axis_dim in range(3):
        flux_pad = field_pad[1 + axis_dim]
        flux_here = neighbor(flux_pad, axis_dim, 0)
        for offset in (1, -1):
            perm_there = neighbor(perm_pad, axis_dim, offset)
            conduct = 2.0 * perm_here * perm_there / (perm_here + perm_there)
            source_flux = offset * 0.5 * (flux_here + neighbor(flux_pad, axis_dim, offset))
            numerator = numerator + conduct * neighbor(padded, axis_dim, offset) - source_flux
            denominator = denominator + conduct
    return numerator / denominator

def reference(source_field, labels):
    weights = chebyshev_weights(ITERS)
    potential = jnp.zeros(labels.shape, jnp.float32)
    earlier = potential
    padded = pad_grid(potential)
    cell_count = labels.shape[0] * labels.shape[1] * labels.shape[2]
    for sweep_index in range(ITERS):
        field_pad = pad_grid(field_terms(padded, source_field, labels))
        relaxed = relax(padded, field_pad)
        update = earlier + weights[sweep_index] * (relaxed - earlier) - potential
        sum_squares = jnp.sum(update * update)
        factor = jnp.minimum(1.0, step_cap / jnp.sqrt(sum_squares / cell_count + 1e-06))
        earlier = potential
        potential = potential + factor * update
        padded = pad_grid(potential)
    return potential
```

```python
import jax
import jax.numpy as jnp
from jax import lax
from jax.experimental import pallas as pl
from jax.experimental.pallas import tpu as pltpu
from jax.sharding import PartitionSpec as P

ITERS = 4
iron_perm = 40.0
iron_sat = 0.25
coil_perm = 4.0
coil_sat = 1.0
step_cap = 0.1
spectral = 0.9
MESH = pl.DeviceIdType.MESH


def chebyshev_weights(sweep_count):
    weights = [1.0]
    weights.append(1.0 / (1.0 - spectral * spectral / 2.0))
    while len(weights) < sweep_count:
        weights.append(1.0 / (1.0 - spectral * spectral * weights[-1] / 4.0))
    return weights


def make_kernel(n_phi, n_row, n_gz, shape):
    s_phi, s_z, s_r = shape
    peers = n_phi * n_row * n_gz
    half = s_phi // 2
    wide = 2 * s_r
    tall = s_z + 8
    cell_count = s_phi * s_z * s_r * peers
    weights = chebyshev_weights(ITERS)
    first, last = 2, half + 1

    def kernel(src, lab, out, S, L, A, B, Pot, M, U, G, FP, FU, sum_sem, halo_send, halo_recv, in_send, in_recv, loc_sem):
        p = lax.axis_index("phi")
        c = lax.axis_index("row")
        g = lax.axis_index("gz")
        me = (p * n_row + c) * n_gz + g
        lanes = pl.ds(pl.multiple_of(c * s_r, s_r), s_r)
        sib = 1 - c

        def own_part(core):
            return pl.ds((half - 1) * core, half + 1), pl.ds(2 - core, half + 1)

        def cut(ref, rows, z):
            return ref.at[:, rows, z, :] if ref is src else ref.at[rows, z, :]

        def land(ref, rows, z):
            return ref.at[:, rows, z, lanes] if ref is S else ref.at[rows, z, lanes]

        whole_z = pl.ds(0, s_z)
        local = []
        for n, (a, b) in enumerate(((src, S), (lab, L))):
            frm, to = own_part(c)
            copy = pltpu.make_async_copy(cut(a, frm, whole_z), land(b, to, whole_z), loc_sem.at[n])
            copy.start()
            local.append(copy)

        def peer(j):
            t = lax.rem(me + j, peers)
            return {"phi": t // (n_row * n_gz), "row": lax.rem(t // n_gz, n_row), "gz": lax.rem(t, n_gz)}

        rim = pl.ds(s_z, 8)
        S[:, :, rim, :] = jnp.zeros((3, half + 4, 8, wide), jnp.float32)
        L[:, rim, :] = jnp.zeros((half + 4, 8, wide), jnp.int32)
        for k in range(ITERS - 1):
            U[k, :, rim, :] = jnp.zeros((half + 4, 8, wide), jnp.float32)

        barrier = pltpu.get_barrier_semaphore()

        def greet(j, carry):
            pl.semaphore_signal(barrier, inc=1, device_id=peer(j), device_id_type=MESH)
            return carry

        lax.fori_loop(1, peers, greet, 0)
        pl.semaphore_wait(barrier, peers - 1)

        up_p, down_p = lax.rem(p + 1, n_phi), lax.rem(p + n_phi - 1, n_phi)
        has_up, has_down = g < n_gz - 1, g > 0
        up_g, down_g = jnp.minimum(g + 1, n_gz - 1), jnp.maximum(g - 1, 0)

        always, when_up, when_down = [], [], []
        for n, (a, b) in enumerate(((src, S), (lab, L))):
            def remote(frm, to, send, recv, where, n=n):
                return pltpu.make_async_remote_copy(
                    src_ref=frm, dst_ref=to, send_sem=in_send.at[n, send], recv_sem=in_recv.at[n, recv],
                    device_id=where, device_id_type=MESH)

            frm, to = own_part(sib)
            always.append(remote(cut(a, pl.ds(s_phi - 1, 1), whole_z), land(b, pl.ds(1, 1), whole_z), 1, 1 + c,
                                 {"phi": up_p, "row": 0}))
            always.append(remote(cut(a, pl.ds(0, 1), whole_z), land(b, pl.ds(last + 1, 1), whole_z), 2, 1 + c,
                                 {"phi": down_p, "row": 1}))
            always.append(remote(cut(a, frm, whole_z), land(b, to, whole_z), 0, 0, {"row": sib}))
            for t in range(2):
                rows = pl.ds(half * t, half)
                when_up.append(remote(cut(a, rows, pl.ds(s_z - 1, 1)), land(b, pl.ds(first, half), pl.ds(tall - 1, 1)),
                                      3 + t, 3 + c, {"gz": up_g, "row": t}))
                when_down.append(remote(cut(a, rows, pl.ds(0, 1)), land(b, pl.ds(first, half), pl.ds(s_z, 1)),
                                        5 + t, 5 + c, {"gz": down_g, "row": t}))

        def start_all(copies):
            for copy in copies:
                copy.start()

        def send_wait_all(copies):
            for copy in copies:
                copy.wait_send()

        @pl.when(has_up)
        def _():
            start_all(when_up)

        @pl.when(has_down)
        def _():
            start_all(when_down)

        start_all(always)

        def arrived(b, n, slot, rows, z, ln):
            ref = b.at[:, rows, z, ln] if b is S else b.at[rows, z, ln]
            pltpu.make_async_remote_copy(
                src_ref=ref, dst_ref=ref, send_sem=in_send.at[n, 0], recv_sem=in_recv.at[n, slot],
                device_id={"row": sib}, device_id_type=MESH).wait_recv()

        for copy in local:
            copy.wait()
        for n, b in enumerate((S, L)):
            frm, to = own_part(c)
            arrived(b, n, 0, to, whole_z, pl.ds(pl.multiple_of(sib * s_r, s_r), s_r))
            for core in range(2):
                arrived(b, n, 1 + core, pl.ds(jnp.where(c == 0, 1, last + 1), 1), whole_z, pl.ds(core * s_r, s_r))

        @pl.when(has_down)
        def _():
            for n, b in enumerate((S, L)):
                for core in range(2):
                    arrived(b, n, 3 + core, pl.ds(first, half), pl.ds(tall - 1, 1), pl.ds(core * s_r, s_r))

        @pl.when(has_up)
        def _():
            for n, b in enumerate((S, L)):
                for core in range(2):
                    arrived(b, n, 5 + core, pl.ds(first, half), pl.ds(s_z, 1), pl.ds(core * s_r, s_r))

        lane = lax.broadcasted_iota(jnp.int32, (tall, wide), 1)
        at_end, at_start = lane == wide - 1, lane == 0

        def z_up(x):
            return pltpu.roll(x, tall - 1, 0)

        def z_down(x):
            return pltpu.roll(x, 1, 0)

        def r_up(x, edge):
            return jnp.where(at_end[: x.shape[0]], edge, pltpu.roll(x, wide - 1, 1))

        def r_down(x, edge):
            return jnp.where(at_start[: x.shape[0]], edge, pltpu.roll(x, 1, 1))

        def conduct(a, b):
            return 2.0 * a * b / (a + b)

        q_up = {"phi": jnp.where(c == 1, up_p, p), "row": sib}
        q_down = {"phi": jnp.where(c == 0, down_p, p), "row": sib}
        z_top, z_low = pl.ds(s_z - 2, 2), pl.ds(0, 2)
        at_low, at_top = pl.ds(tall - 2, 2), pl.ds(s_z, 2)

        def halo(k, slot):
            def ref(rows, z):
                return U.at[k, rows, z, :]

            own = pl.ds(first, half)
            frm, to, where = (
                (ref(pl.ds(last - 1, 2), whole_z), ref(pl.ds(0, 2), whole_z), q_up),
                (ref(pl.ds(first, 2), whole_z), ref(pl.ds(last + 1, 2), whole_z), q_down),
                (ref(own, z_top), ref(own, at_low), {"gz": up_g}),
                (ref(own, z_low), ref(own, at_top), {"gz": down_g}),
                (ref(pl.ds(last, 1), z_top), ref(pl.ds(1, 1), at_low), dict(q_up, gz=up_g)),
                (ref(pl.ds(first, 1), z_top), ref(pl.ds(last + 1, 1), at_low), dict(q_down, gz=up_g)),
                (ref(pl.ds(last, 1), z_low), ref(pl.ds(1, 1), at_top), dict(q_up, gz=down_g)),
                (ref(pl.ds(first, 1), z_low), ref(pl.ds(last + 1, 1), at_top), dict(q_down, gz=down_g)),
            )[slot]
            return pltpu.make_async_remote_copy(
                src_ref=frm, dst_ref=to, send_sem=halo_send.at[k, slot], recv_sem=halo_recv.at[k, slot],
                device_id=where, device_id_type=MESH)

        UP, DOWN, BOTH = (2, 4, 5), (3, 6, 7), (0, 1)

        def halo_start(k):
            @pl.when(has_up)
            def _():
                start_all([halo(k, s) for s in UP])

            @pl.when(has_down)
            def _():
                start_all([halo(k, s) for s in DOWN])

            start_all([halo(k, s) for s in BOTH])

        def halo_arrive(k):
            for s in BOTH:
                halo(k, s).wait_recv()

            @pl.when(has_down)
            def _():
                for s in UP:
                    halo(k, s).wait_recv()

            @pl.when(has_up)
            def _():
                for s in DOWN:
                    halo(k, s).wait_recv()

        def halo_sent(k):
            send_wait_all([halo(k, s) for s in BOTH])

            @pl.when(has_up)
            def _():
                send_wait_all([halo(k, s) for s in UP])

            @pl.when(has_down)
            def _():
                send_wait_all([halo(k, s) for s in DOWN])

        def swap(frm, to, slot):
            return pltpu.make_async_remote_copy(
                src_ref=frm, dst_ref=to, send_sem=halo_send.at[ITERS - 1, slot], recv_sem=halo_recv.at[ITERS - 1, slot],
                device_id={"row": sib}, device_id_type=MESH)

        other_lanes = pl.ds(pl.multiple_of(sib * s_r, s_r), s_r)
        own_rows = pl.ds(first, half)

        def total_wait(k):
            return pltpu.make_async_remote_copy(
                src_ref=G.at[k, pl.ds(1, peers - 1)], dst_ref=G.at[k, pl.ds(1, peers - 1)],
                send_sem=sum_sem.at[0, k], recv_sem=sum_sem.at[1, k], device_id={"row": sib}, device_id_type=MESH)

        for k in range(ITERS):
            cur = k % 2

            def perm_row(i, carry, k=k, cur=cur):
                if k == 0:
                    label = L[i]
                    a = jnp.where(label == 1, iron_perm - 1.0, jnp.where(label == 2, coil_perm - 1.0, 0.0))
                    b = jnp.where(label == 1, 1.0 / iron_sat, jnp.where(label == 2, 1.0 / coil_sat, 0.0))
                    A[i] = a
                    B[i] = b
                    s0, s1, s2 = S[0, i], S[1, i], S[2, i]
                else:
                    a, b = A[i], B[i]
                    here = Pot[cur, i]
                    s0 = S[0, i] - 0.5 * (Pot[cur, i + 1] - Pot[cur, i - 1])
                    s1 = S[1, i] - 0.5 * (z_up(here) - z_down(here))
                    s2 = S[2, i] - 0.5 * (r_up(here, 0.0) - r_down(here, 0.0))
                field_sq = s0 * s0 + s1 * s1 + s2 * s2
                M[i] = 1.0 + a / (1.0 + field_sq * b)
                return carry

            lax.fori_loop(1, half + 3, perm_row, 0)

            def relax_row(i, carry, k=k, cur=cur):
                below, acc = carry
                m = M[i]
                mi = m[:s_z]
                above = conduct(mi, M[i + 1, :s_z])
                cz = conduct(m, z_up(m))
                cz_low = z_down(cz)[:s_z]
                cz = cz[:s_z]
                cr = conduct(mi, r_up(mi, 1.0))
                cr_low = conduct(mi, r_down(mi, 1.0))
                fz = m * S[1, i]
                fr = mi * S[2, i, :s_z]
                flux = M[i + 1, :s_z] * S[0, i + 1, :s_z] - M[i - 1, :s_z] * S[0, i - 1, :s_z]
                flux = flux + (z_up(fz) - z_down(fz))[:s_z] + (r_up(fr, 0.0) - r_down(fr, 0.0))
                numerator = -0.5 * flux
                if k > 0:
                    here = Pot[cur, i]
                    hi = here[:s_z]
                    numerator = (numerator + above * Pot[cur, i + 1, :s_z] + below * Pot[cur, i - 1, :s_z]
                                 + cz * z_up(here)[:s_z] + cz_low * z_down(here)[:s_z]
                                 + cr * r_up(hi, 0.0) + cr_low * r_down(hi, 0.0))
                relaxed = numerator / (above + below + cz + cz_low + cr + cr_low)
                if k == 0:
                    update = weights[0] * relaxed
                elif k == 1:
                    update = weights[1] * relaxed - hi
                else:
                    earlier = Pot[1 - cur, i, :s_z]
                    update = earlier + weights[k] * (relaxed - earlier) - hi
                U[k, i, :s_z] = update
                return above, acc + update * update

            start = conduct(M[1, :s_z], M[2, :s_z])
            _, acc = lax.fori_loop(first, last + 1, relax_row, (start, jnp.zeros((s_z, wide), jnp.float32)))

            if k < ITERS - 1:
                halo_start(k)
            else:
                give_update = swap(U.at[k, own_rows, whole_z, other_lanes], FU, 1)
                give_update.start()
            acc = acc[:, :s_r] + acc[:, s_r:]
            part = acc[:8]
            for z in range(8, s_z, 8):
                part = part + acc[z : z + 8]
            G[k, 0] = part

            def share(j, carry, k=k):
                pltpu.make_async_remote_copy(
                    src_ref=G.at[k, 0], dst_ref=G.at[k, peers - j], send_sem=sum_sem.at[0, k],
                    recv_sem=sum_sem.at[1, k], device_id=peer(j), device_id_type=MESH).start()
                return carry

            lax.fori_loop(1, peers, share, 0)
            total_wait(k).wait_recv()
            sum_squares = jnp.sum(jnp.sum(G[k], axis=0), keepdims=True)
            factor = jnp.minimum(1.0, step_cap / jnp.sqrt(sum_squares / cell_count + 1e-06))

            if k < ITERS - 1:
                halo_arrive(k)
                wide_factor = jnp.broadcast_to(factor, (tall, wide))

                def step(i, carry, k=k, cur=cur):
                    new = wide_factor * U[k, i]
                    if k > 0:
                        new = new + Pot[cur, i]
                    Pot[1 - cur, i] = new
                    return carry

                lax.fori_loop(0, half + 4, step, 0)
                if k == ITERS - 2:
                    give_potential = swap(Pot.at[1 - cur, own_rows, whole_z, other_lanes], FP, 0)
                    give_potential.start()
            else:
                wide_factor = jnp.broadcast_to(factor, (half, s_z, s_r))
                out[pl.ds(half * c, half)] = (
                    Pot[cur, first : last + 1, :s_z, lanes] + wide_factor * U[k, first : last + 1, :s_z, lanes])
                give_potential.wait_recv()
                give_update.wait_recv()
                out[pl.ds(half * sib, half)] = FP[...] + wide_factor * FU[...]

        send_wait_all(always)

        @pl.when(has_up)
        def _():
            send_wait_all(when_up)

        @pl.when(has_down)
        def _():
            send_wait_all(when_down)

        for k in range(ITERS):
            total_wait(k).wait_send()
            if k < ITERS - 1:
                halo_sent(k)
        give_potential.wait_send()
        give_update.wait_send()

    rows = half + 4
    scratch = [
        pltpu.VMEM((3, rows, tall, wide), jnp.float32),
        pltpu.VMEM((rows, tall, wide), jnp.int32),
        pltpu.VMEM((rows, tall, wide), jnp.float32),
        pltpu.VMEM((rows, tall, wide), jnp.float32),
        pltpu.VMEM((2, rows, tall, wide), jnp.float32),
        pltpu.VMEM((rows, tall, wide), jnp.float32),
        pltpu.VMEM((ITERS, rows, tall, wide), jnp.float32),
        pltpu.VMEM((ITERS, peers, 8, s_r), jnp.float32),
        pltpu.VMEM((half, s_z, s_r), jnp.float32),
        pltpu.VMEM((half, s_z, s_r), jnp.float32),
        pltpu.SemaphoreType.DMA((2, ITERS)),
        pltpu.SemaphoreType.DMA((ITERS, 8)),
        pltpu.SemaphoreType.DMA((ITERS, 8)),
        pltpu.SemaphoreType.DMA((2, 7)),
        pltpu.SemaphoreType.DMA((2, 7)),
        pltpu.SemaphoreType.DMA((2,)),
    ]
    return pl.pallas_call(
        kernel,
        out_shape=jax.ShapeDtypeStruct(shape, jnp.float32),
        in_specs=[pl.BlockSpec(memory_space=pl.ANY)] * 2,
        out_specs=pl.BlockSpec(memory_space=pltpu.VMEM),
        scratch_shapes=scratch,
        compiler_params=pltpu.CompilerParams(
            collective_id=0, has_side_effects=True, vmem_limit_bytes=24 * 1024 * 1024),
        name="sweeps",
    )


def solution(mesh):
    sizes = mesh.shape

    def on_device(source_field, labels):
        return make_kernel(sizes["phi"], sizes["row"], sizes["gz"], labels.shape)(source_field, labels)

    placed = (P(None, ("group", "phi"), "gz", "row"), P(("group", "phi"), "gz", "row"))
    return jax.shard_map(
        on_device,
        mesh=mesh,
        in_specs=placed,
        out_specs=P(("group", "phi"), "gz", "row"),
        check_vma=False,
    )
```

```python
import jax
import jax.numpy as jnp
from jax import lax
from jax.experimental import pallas as pl
from jax.experimental.pallas import tpu as pltpu
from jax.sharding import PartitionSpec as P

ITERS = 4
iron_perm = 40.0
iron_sat = 0.25
coil_perm = 4.0
coil_sat = 1.0
step_cap = 0.1
spectral = 0.9
MESH = pl.DeviceIdType.MESH


def chebyshev_weights(sweep_count):
    weights = [1.0]
    weights.append(1.0 / (1.0 - spectral * spectral / 2.0))
    while len(weights) < sweep_count:
        weights.append(1.0 / (1.0 - spectral * spectral * weights[-1] / 4.0))
    return weights


def make_kernel(n_phi, n_row, n_gz, shape):
    s_phi, s_z, s_r = shape
    peers = n_phi * n_row * n_gz
    half = s_phi // 2
    wide = 2 * s_r
    tall = s_z + 8
    cell_count = s_phi * s_z * s_r * peers
    weights = chebyshev_weights(ITERS)
    first, last = 2, half + 1

    def kernel(src, lab, out, S, L, A, B, Pot, M, U, G, FP, FU, X, XL, sum_sem, halo_send, halo_recv, in_send, in_recv, loc_sem):
        p = lax.axis_index("phi")
        c = lax.axis_index("row")
        g = lax.axis_index("gz")
        lanes = pl.ds(pl.multiple_of(c * s_r, s_r), s_r)
        sib = 1 - c

        def own_part(core):
            return pl.ds((half - 1) * core, half + 1), pl.ds(2 - core, half + 1)

        def cut(ref, rows, z):
            return ref.at[:, rows, z, :] if ref is src or ref is X else ref.at[rows, z, :]

        def land(ref, rows, z):
            return ref.at[:, rows, z, lanes] if ref is S else ref.at[rows, z, lanes]

        whole_z = pl.ds(0, s_z)
        local, stages = [], []
        for n, (a, b, staged) in enumerate(((src, S, X), (lab, L, XL))):
            stage = pltpu.make_async_copy(a, staged, loc_sem.at[2 + n])
            stage.start()
            stages.append(stage)
            frm, to = own_part(c)
            copy = pltpu.make_async_copy(cut(a, frm, whole_z), land(b, to, whole_z), loc_sem.at[n])
            copy.start()
            local.append(copy)

        def peer(j):
            return {
                "phi": lax.rem(p + j // (n_row * n_gz), n_phi),
                "row": lax.rem(c + (j // n_gz) % n_row, n_row),
                "gz": lax.rem(g + j % n_gz, n_gz),
            }

        def each_peer(body):
            if peers > 32:
                lax.fori_loop(1, peers, lambda j, carry: (body(j, peer(j)), carry)[1], 0)
            else:
                for j, where in peer_list:
                    body(j, where)

        if peers <= 32:
            per_chip = n_row * n_gz
            order = sorted(range(1, peers), key=lambda j: -min(j // per_chip, n_phi - j // per_chip))
            peer_list = [(j, peer(j)) for j in order]

        rim = pl.ds(s_z, 8)
        S[:, :, rim, :] = jnp.zeros((3, half + 4, 8, wide), jnp.float32)
        L[:, rim, :] = jnp.zeros((half + 4, 8, wide), jnp.int32)
        for k in range(ITERS - 1):
            U[k, :, rim, :] = jnp.zeros((half + 4, 8, wide), jnp.float32)

        barrier = pltpu.get_barrier_semaphore()

        def greet(j, where):
            pl.semaphore_signal(barrier, inc=1, device_id=where, device_id_type=MESH)

        each_peer(greet)
        pl.semaphore_wait(barrier, peers - 1)

        for stage in stages:
            stage.wait()
        up_p, down_p = lax.rem(p + 1, n_phi), lax.rem(p + n_phi - 1, n_phi)
        has_up, has_down = g < n_gz - 1, g > 0
        up_g, down_g = jnp.minimum(g + 1, n_gz - 1), jnp.maximum(g - 1, 0)

        always, when_up, when_down = [], [], []
        for n, (a, b) in enumerate(((X, S), (XL, L))):
            def remote(frm, to, send, recv, where, n=n):
                return pltpu.make_async_remote_copy(
                    src_ref=frm, dst_ref=to, send_sem=in_send.at[n, send], recv_sem=in_recv.at[n, recv],
                    device_id=where, device_id_type=MESH)

            frm, to = own_part(sib)
            always.append(remote(cut(a, pl.ds(s_phi - 1, 1), whole_z), land(b, pl.ds(1, 1), whole_z), 1, 1 + c,
                                 {"phi": up_p, "row": 0}))
            always.append(remote(cut(a, pl.ds(0, 1), whole_z), land(b, pl.ds(last + 1, 1), whole_z), 2, 1 + c,
                                 {"phi": down_p, "row": 1}))
            always.append(remote(cut(a, frm, whole_z), land(b, to, whole_z), 0, 0, {"row": sib}))
            for t in range(2):
                rows = pl.ds(half * t, half)
                when_up.append(remote(cut(a, rows, pl.ds(s_z - 1, 1)), land(b, pl.ds(first, half), pl.ds(tall - 1, 1)),
                                      3 + t, 3 + c, {"gz": up_g, "row": t}))
                when_down.append(remote(cut(a, rows, pl.ds(0, 1)), land(b, pl.ds(first, half), pl.ds(s_z, 1)),
                                        5 + t, 5 + c, {"gz": down_g, "row": t}))

        def start_all(copies):
            for copy in copies:
                copy.start()

        def send_wait_all(copies):
            for copy in copies:
                copy.wait_send()

        @pl.when(has_up)
        def _():
            start_all(when_up)

        @pl.when(has_down)
        def _():
            start_all(when_down)

        start_all(always)

        def arrived(b, n, slot, rows, z, ln):
            ref = b.at[:, rows, z, ln] if b is S else b.at[rows, z, ln]
            pltpu.make_async_remote_copy(
                src_ref=ref, dst_ref=ref, send_sem=in_send.at[n, 0], recv_sem=in_recv.at[n, slot],
                device_id={"row": sib}, device_id_type=MESH).wait_recv()

        for copy in local:
            copy.wait()
        for n, b in enumerate((S, L)):
            frm, to = own_part(c)
            arrived(b, n, 0, to, whole_z, pl.ds(pl.multiple_of(sib * s_r, s_r), s_r))
            for core in range(2):
                arrived(b, n, 1 + core, pl.ds(jnp.where(c == 0, 1, last + 1), 1), whole_z, pl.ds(core * s_r, s_r))

        @pl.when(has_down)
        def _():
            for n, b in enumerate((S, L)):
                for core in range(2):
                    arrived(b, n, 3 + core, pl.ds(first, half), pl.ds(tall - 1, 1), pl.ds(core * s_r, s_r))

        @pl.when(has_up)
        def _():
            for n, b in enumerate((S, L)):
                for core in range(2):
                    arrived(b, n, 5 + core, pl.ds(first, half), pl.ds(s_z, 1), pl.ds(core * s_r, s_r))

        lane = lax.broadcasted_iota(jnp.int32, (tall, wide), 1)
        at_end, at_start = lane == wide - 1, lane == 0

        def z_up(x):
            return pltpu.roll(x, tall - 1, 0)

        def z_down(x):
            return pltpu.roll(x, 1, 0)

        def r_up(x, edge):
            return jnp.where(at_end[: x.shape[0]], edge, pltpu.roll(x, wide - 1, 1))

        def r_down(x, edge):
            return jnp.where(at_start[: x.shape[0]], edge, pltpu.roll(x, 1, 1))

        def conduct(a, b):
            return 2.0 * a * b / (a + b)

        q_up = {"phi": jnp.where(c == 1, up_p, p), "row": sib}
        q_down = {"phi": jnp.where(c == 0, down_p, p), "row": sib}
        z_top, z_low = pl.ds(s_z - 2, 2), pl.ds(0, 2)
        at_low, at_top = pl.ds(tall - 2, 2), pl.ds(s_z, 2)

        def halo(k, slot):
            def ref(rows, z):
                return U.at[k, rows, z, :]

            own = pl.ds(first, half)
            frm, to, where = (
                (ref(pl.ds(last - 1, 2), whole_z), ref(pl.ds(0, 2), whole_z), q_up),
                (ref(pl.ds(first, 2), whole_z), ref(pl.ds(last + 1, 2), whole_z), q_down),
                (ref(own, z_top), ref(own, at_low), {"gz": up_g}),
                (ref(own, z_low), ref(own, at_top), {"gz": down_g}),
                (ref(pl.ds(last, 1), z_top), ref(pl.ds(1, 1), at_low), dict(q_up, gz=up_g)),
                (ref(pl.ds(first, 1), z_top), ref(pl.ds(last + 1, 1), at_low), dict(q_down, gz=up_g)),
                (ref(pl.ds(last, 1), z_low), ref(pl.ds(1, 1), at_top), dict(q_up, gz=down_g)),
                (ref(pl.ds(first, 1), z_low), ref(pl.ds(last + 1, 1), at_top), dict(q_down, gz=down_g)),
            )[slot]
            return pltpu.make_async_remote_copy(
                src_ref=frm, dst_ref=to, send_sem=halo_send.at[k, slot], recv_sem=halo_recv.at[k, slot],
                device_id=where, device_id_type=MESH)

        UP, DOWN, BOTH = (2, 4, 5), (3, 6, 7), (0, 1)

        def halo_start(k):
            @pl.when(has_up)
            def _():
                start_all([halo(k, s) for s in UP])

            @pl.when(has_down)
            def _():
                start_all([halo(k, s) for s in DOWN])

            start_all([halo(k, s) for s in BOTH])

        def halo_arrive(k):
            for s in BOTH:
                halo(k, s).wait_recv()

            @pl.when(has_down)
            def _():
                for s in UP:
                    halo(k, s).wait_recv()

            @pl.when(has_up)
            def _():
                for s in DOWN:
                    halo(k, s).wait_recv()

        def halo_sent(k):
            send_wait_all([halo(k, s) for s in BOTH])

            @pl.when(has_up)
            def _():
                send_wait_all([halo(k, s) for s in UP])

            @pl.when(has_down)
            def _():
                send_wait_all([halo(k, s) for s in DOWN])

        def swap(frm, to, slot):
            return pltpu.make_async_remote_copy(
                src_ref=frm, dst_ref=to, send_sem=halo_send.at[ITERS - 1, slot], recv_sem=halo_recv.at[ITERS - 1, slot],
                device_id={"row": sib}, device_id_type=MESH)

        other_lanes = pl.ds(pl.multiple_of(sib * s_r, s_r), s_r)
        own_rows = pl.ds(first, half)

        def total_wait(k):
            return pltpu.make_async_remote_copy(
                src_ref=G.at[k, pl.ds(1, peers - 1)], dst_ref=G.at[k, pl.ds(1, peers - 1)],
                send_sem=sum_sem.at[0, k], recv_sem=sum_sem.at[1, k], device_id={"row": sib}, device_id_type=MESH)

        for k in range(ITERS):
            cur = k % 2

            def perm_row(i, carry, k=k, cur=cur):
                if k == 0:
                    label = L[i]
                    a = jnp.where(label == 1, iron_perm - 1.0, jnp.where(label == 2, coil_perm - 1.0, 0.0))
                    b = jnp.where(label == 1, 1.0 / iron_sat, jnp.where(label == 2, 1.0 / coil_sat, 0.0))
                    A[i] = a
                    B[i] = b
                    s0, s1, s2 = S[0, i], S[1, i], S[2, i]
                else:
                    a, b = A[i], B[i]
                    here = Pot[cur, i]
                    s0 = S[0, i] - 0.5 * (Pot[cur, i + 1] - Pot[cur, i - 1])
                    s1 = S[1, i] - 0.5 * (z_up(here) - z_down(here))
                    s2 = S[2, i] - 0.5 * (r_up(here, 0.0) - r_down(here, 0.0))
                field_sq = s0 * s0 + s1 * s1 + s2 * s2
                M[i] = 1.0 + a / (1.0 + field_sq * b)
                return carry

            lax.fori_loop(1, half + 3, perm_row, 0, unroll=True)

            def relax_row(i, carry, k=k, cur=cur):
                below, acc = carry
                m = M[i]
                mi = m[:s_z]
                above = conduct(mi, M[i + 1, :s_z])
                cz = conduct(m, z_up(m))
                cz_low = z_down(cz)[:s_z]
                cz = cz[:s_z]
                cr = conduct(mi, r_up(mi, 1.0))
                cr_low = conduct(mi, r_down(mi, 1.0))
                fz = m * S[1, i]
                fr = mi * S[2, i, :s_z]
                flux = M[i + 1, :s_z] * S[0, i + 1, :s_z] - M[i - 1, :s_z] * S[0, i - 1, :s_z]
                flux = flux + (z_up(fz) - z_down(fz))[:s_z] + (r_up(fr, 0.0) - r_down(fr, 0.0))
                numerator = -0.5 * flux
                if k > 0:
                    here = Pot[cur, i]
                    hi = here[:s_z]
                    numerator = (numerator + above * Pot[cur, i + 1, :s_z] + below * Pot[cur, i - 1, :s_z]
                                 + cz * z_up(here)[:s_z] + cz_low * z_down(here)[:s_z]
                                 + cr * r_up(hi, 0.0) + cr_low * r_down(hi, 0.0))
                relaxed = numerator / (above + below + cz + cz_low + cr + cr_low)
                if k == 0:
                    update = weights[0] * relaxed
                elif k == 1:
                    update = weights[1] * relaxed - hi
                else:
                    earlier = Pot[1 - cur, i, :s_z]
                    update = earlier + weights[k] * (relaxed - earlier) - hi
                U[k, i, :s_z] = update
                return above, acc + update * update

            start = conduct(M[1, :s_z], M[2, :s_z])
            _, acc = lax.fori_loop(first, last + 1, relax_row, (start, jnp.zeros((s_z, wide), jnp.float32)), unroll=True)

            if k < ITERS - 1:
                halo_start(k)
            else:
                give_update = swap(U.at[k, own_rows, whole_z, other_lanes], FU, 1)
                give_update.start()
            acc = acc[:, :s_r] + acc[:, s_r:]
            part = acc[:8]
            for z in range(8, s_z, 8):
                part = part + acc[z : z + 8]
            G[k, 0:1] = jnp.sum(part, axis=0, keepdims=True)

            def share(j, where, k=k):
                pltpu.make_async_remote_copy(
                    src_ref=G.at[k, pl.ds(0, 1)], dst_ref=G.at[k, pl.ds(j, 1)], send_sem=sum_sem.at[0, k],
                    recv_sem=sum_sem.at[1, k], device_id=where, device_id_type=MESH).start()

            each_peer(share)
            total_wait(k).wait_recv()
            sum_squares = jnp.sum(jnp.sum(G[k], axis=0, keepdims=True), axis=1, keepdims=True)
            factor = jnp.minimum(1.0, step_cap * lax.rsqrt(sum_squares * (1.0 / cell_count) + 1e-06))

            if k < ITERS - 1:
                halo_arrive(k)
                wide_factor = jnp.broadcast_to(factor, (tall, wide))

                def step(i, carry, k=k, cur=cur):
                    new = wide_factor * U[k, i]
                    if k > 0:
                        new = new + Pot[cur, i]
                    Pot[1 - cur, i] = new
                    return carry

                lax.fori_loop(0, half + 4, step, 0, unroll=True)
                if k == ITERS - 2:
                    give_potential = swap(Pot.at[1 - cur, own_rows, whole_z, other_lanes], FP, 0)
                    give_potential.start()
            else:
                wide_factor = jnp.broadcast_to(factor, (half, s_z, s_r))
                out[pl.ds(half * c, half)] = (
                    Pot[cur, first : last + 1, :s_z, lanes] + wide_factor * U[k, first : last + 1, :s_z, lanes])
                give_potential.wait_recv()
                give_update.wait_recv()
                out[pl.ds(half * sib, half)] = FP[...] + wide_factor * FU[...]

        send_wait_all(always)

        @pl.when(has_up)
        def _():
            send_wait_all(when_up)

        @pl.when(has_down)
        def _():
            send_wait_all(when_down)

        for k in range(ITERS):
            total_wait(k).wait_send()
            if k < ITERS - 1:
                halo_sent(k)
        give_potential.wait_send()
        give_update.wait_send()

    rows = half + 4
    scratch = [
        pltpu.VMEM((3, rows, tall, wide), jnp.float32),
        pltpu.VMEM((rows, tall, wide), jnp.int32),
        pltpu.VMEM((rows, tall, wide), jnp.float32),
        pltpu.VMEM((rows, tall, wide), jnp.float32),
        pltpu.VMEM((2, rows, tall, wide), jnp.float32),
        pltpu.VMEM((rows, tall, wide), jnp.float32),
        pltpu.VMEM((ITERS, rows, tall, wide), jnp.float32),
        pltpu.VMEM((ITERS, peers, s_r), jnp.float32),
        pltpu.VMEM((half, s_z, s_r), jnp.float32),
        pltpu.VMEM((half, s_z, s_r), jnp.float32),
        pltpu.VMEM((3,) + tuple(shape), jnp.float32),
        pltpu.VMEM(tuple(shape), jnp.int32),
        pltpu.SemaphoreType.DMA((2, ITERS)),
        pltpu.SemaphoreType.DMA((ITERS, 8)),
        pltpu.SemaphoreType.DMA((ITERS, 8)),
        pltpu.SemaphoreType.DMA((2, 7)),
        pltpu.SemaphoreType.DMA((2, 7)),
        pltpu.SemaphoreType.DMA((4,)),
    ]
    return pl.pallas_call(
        kernel,
        out_shape=jax.ShapeDtypeStruct(shape, jnp.float32),
        in_specs=[pl.BlockSpec(memory_space=pltpu.HBM)] * 2,
        out_specs=pl.BlockSpec(memory_space=pltpu.VMEM),
        scratch_shapes=scratch,
        compiler_params=pltpu.CompilerParams(
            collective_id=0, has_side_effects=True, vmem_limit_bytes=24 * 1024 * 1024),
        name="sweeps",
    )


def solution(mesh):
    sizes = mesh.shape

    def on_device(source_field, labels):
        return make_kernel(sizes["phi"], sizes["row"], sizes["gz"], labels.shape)(source_field, labels)

    placed = (P(None, ("group", "phi"), "gz", "row"), P(("group", "phi"), "gz", "row"))
    return jax.shard_map(
        on_device,
        mesh=mesh,
        in_specs=placed,
        out_specs=P(("group", "phi"), "gz", "row"),
        check_vma=False,
    )
```

```python
import jax
import jax.numpy as jnp
from jax import lax
from jax.experimental import pallas as pl
from jax.experimental.pallas import tpu as pltpu
from jax.sharding import PartitionSpec as P

ITERS = 4
iron_perm = 40.0
iron_sat = 0.25
coil_perm = 4.0
coil_sat = 1.0
step_cap = 0.1
spectral = 0.9
MESH = pl.DeviceIdType.MESH


def chebyshev_weights(sweep_count):
    weights = [1.0]
    weights.append(1.0 / (1.0 - spectral * spectral / 2.0))
    while len(weights) < sweep_count:
        weights.append(1.0 / (1.0 - spectral * spectral * weights[-1] / 4.0))
    return weights


def make_kernel(n_phi, n_row, n_gz, shape):
    s_phi, s_z, s_r = shape
    peers = n_phi * n_row * n_gz
    half = s_phi // 2
    wide = 2 * s_r
    tall = s_z + 8
    cell_count = s_phi * s_z * s_r * peers
    weights = chebyshev_weights(ITERS)
    first, last = 2, half + 1

    def kernel(src, lab, out, S, L, A, B, Pot, M, U, G, FP, FU, X, XL, sum_sem, halo_send, halo_recv, in_send, in_recv, loc_sem):
        p = lax.axis_index("phi")
        c = lax.axis_index("row")
        g = lax.axis_index("gz")
        lanes = pl.ds(pl.multiple_of(c * s_r, s_r), s_r)
        sib = 1 - c

        def own_part(core):
            return pl.ds((half - 1) * core, half + 1), pl.ds(2 - core, half + 1)

        def cut(ref, rows, z):
            return ref.at[:, rows, z, :] if ref is src or ref is X else ref.at[rows, z, :]

        def land(ref, rows, z):
            return ref.at[:, rows, z, lanes] if ref is S else ref.at[rows, z, lanes]

        whole_z = pl.ds(0, s_z)
        local, stages = [], []
        for n, (a, b, staged) in enumerate(((src, S, X), (lab, L, XL))):
            stage = pltpu.make_async_copy(a, staged, loc_sem.at[2 + n])
            stage.start()
            stages.append(stage)
            frm, to = own_part(c)
            copy = pltpu.make_async_copy(cut(a, frm, whole_z), land(b, to, whole_z), loc_sem.at[n])
            copy.start()
            local.append(copy)

        def peer(j):
            return {
                "phi": lax.rem(p + j // (n_row * n_gz), n_phi),
                "row": lax.rem(c + (j // n_gz) % n_row, n_row),
                "gz": lax.rem(g + j % n_gz, n_gz),
            }

        def each_peer(body):
            if peers > 32:
                lax.fori_loop(1, peers, lambda j, carry: (body(j, peer(j)), carry)[1], 0)
            else:
                for j, where in peer_list:
                    body(j, where)

        if peers <= 32:
            per_chip = n_row * n_gz
            order = sorted(range(1, peers), key=lambda j: -min(j // per_chip, n_phi - j // per_chip))
            peer_list = [(j, peer(j)) for j in order]

        rim = pl.ds(s_z, 8)
        S[:, :, rim, :] = jnp.zeros((3, half + 4, 8, wide), jnp.float32)
        L[:, rim, :] = jnp.zeros((half + 4, 8, wide), jnp.int32)
        for k in range(ITERS - 1):
            U[k, :, rim, :] = jnp.zeros((half + 4, 8, wide), jnp.float32)

        barrier = pltpu.get_barrier_semaphore()

        def greet(j, where):
            pl.semaphore_signal(barrier, inc=1, device_id=where, device_id_type=MESH)

        each_peer(greet)
        pl.semaphore_wait(barrier, peers - 1)

        for stage in stages:
            stage.wait()
        up_p, down_p = lax.rem(p + 1, n_phi), lax.rem(p + n_phi - 1, n_phi)
        has_up, has_down = g < n_gz - 1, g > 0
        up_g, down_g = jnp.minimum(g + 1, n_gz - 1), jnp.maximum(g - 1, 0)

        always, when_up, when_down = [], [], []
        for n, (a, b) in enumerate(((X, S), (XL, L))):
            def remote(frm, to, send, recv, where, n=n):
                return pltpu.make_async_remote_copy(
                    src_ref=frm, dst_ref=to, send_sem=in_send.at[n, send], recv_sem=in_recv.at[n, recv],
                    device_id=where, device_id_type=MESH)

            frm, to = own_part(sib)
            always.append(remote(cut(a, pl.ds(s_phi - 1, 1), whole_z), land(b, pl.ds(1, 1), whole_z), 1, 1 + c,
                                 {"phi": up_p, "row": 0}))
            always.append(remote(cut(a, pl.ds(0, 1), whole_z), land(b, pl.ds(last + 1, 1), whole_z), 2, 1 + c,
                                 {"phi": down_p, "row": 1}))
            always.append(remote(cut(a, frm, whole_z), land(b, to, whole_z), 0, 0, {"row": sib}))
            for t in range(2):
                rows = pl.ds(half * t, half)
                when_up.append(remote(cut(a, rows, pl.ds(s_z - 1, 1)), land(b, pl.ds(first, half), pl.ds(tall - 1, 1)),
                                      3 + t, 3 + c, {"gz": up_g, "row": t}))
                when_down.append(remote(cut(a, rows, pl.ds(0, 1)), land(b, pl.ds(first, half), pl.ds(s_z, 1)),
                                        5 + t, 5 + c, {"gz": down_g, "row": t}))

        def start_all(copies):
            for copy in copies:
                copy.start()

        def send_wait_all(copies):
            for copy in copies:
                copy.wait_send()

        start_all(always)

        @pl.when(has_up)
        def _():
            start_all(when_up)

        @pl.when(has_down)
        def _():
            start_all(when_down)

        def arrived(b, n, slot, rows, z, ln):
            ref = b.at[:, rows, z, ln] if b is S else b.at[rows, z, ln]
            pltpu.make_async_remote_copy(
                src_ref=ref, dst_ref=ref, send_sem=in_send.at[n, 0], recv_sem=in_recv.at[n, slot],
                device_id={"row": sib}, device_id_type=MESH).wait_recv()

        def first_perm(i, z):
            label = L[i, z]
            a = jnp.where(label == 1, iron_perm - 1.0, jnp.where(label == 2, coil_perm - 1.0, 0.0))
            b = jnp.where(label == 1, 1.0 / iron_sat, jnp.where(label == 2, 1.0 / coil_sat, 0.0))
            A[i, z] = a
            B[i, z] = b
            s0, s1, s2 = S[0, i, z], S[1, i, z], S[2, i, z]
            M[i, z] = 1.0 + a / (1.0 + (s0 * s0 + s1 * s1 + s2 * s2) * b)

        for copy in local:
            copy.wait()
        for n, b in enumerate((S, L)):
            arrived(b, n, 0, own_part(c)[1], whole_z, pl.ds(pl.multiple_of(sib * s_r, s_r), s_r))
        for i in range(first, last + 1):
            first_perm(i, whole_z)
        near = jnp.where(c == 0, last + 1, 1)
        first_perm(near, whole_z)
        for n, b in enumerate((S, L)):
            for core in range(2):
                arrived(b, n, 1 + core, pl.ds(jnp.where(c == 0, 1, last + 1), 1), whole_z, pl.ds(core * s_r, s_r))
        first_perm(last + 2 - near, whole_z)

        @pl.when(has_down)
        def _():
            for n, b in enumerate((S, L)):
                for core in range(2):
                    arrived(b, n, 3 + core, pl.ds(first, half), pl.ds(tall - 1, 1), pl.ds(core * s_r, s_r))

        @pl.when(has_up)
        def _():
            for n, b in enumerate((S, L)):
                for core in range(2):
                    arrived(b, n, 5 + core, pl.ds(first, half), pl.ds(s_z, 1), pl.ds(core * s_r, s_r))

        for i in range(1, last + 2):
            first_perm(i, rim)

        lane = lax.broadcasted_iota(jnp.int32, (tall, wide), 1)
        at_end, at_start = lane == wide - 1, lane == 0

        def z_up(x):
            return pltpu.roll(x, tall - 1, 0)

        def z_down(x):
            return pltpu.roll(x, 1, 0)

        def r_up(x, edge):
            return jnp.where(at_end[: x.shape[0]], edge, pltpu.roll(x, wide - 1, 1))

        def r_down(x, edge):
            return jnp.where(at_start[: x.shape[0]], edge, pltpu.roll(x, 1, 1))

        def conduct(a, b):
            return 2.0 * a * b / (a + b)

        q_up = {"phi": jnp.where(c == 1, up_p, p), "row": sib}
        q_down = {"phi": jnp.where(c == 0, down_p, p), "row": sib}
        z_top, z_low = pl.ds(s_z - 2, 2), pl.ds(0, 2)
        at_low, at_top = pl.ds(tall - 2, 2), pl.ds(s_z, 2)

        def halo(k, slot):
            def ref(rows, z):
                return U.at[k, rows, z, :]

            own = pl.ds(first, half)
            frm, to, where = (
                (ref(pl.ds(last - 1, 2), whole_z), ref(pl.ds(0, 2), whole_z), q_up),
                (ref(pl.ds(first, 2), whole_z), ref(pl.ds(last + 1, 2), whole_z), q_down),
                (ref(own, z_top), ref(own, at_low), {"gz": up_g}),
                (ref(own, z_low), ref(own, at_top), {"gz": down_g}),
                (ref(pl.ds(last, 1), z_top), ref(pl.ds(1, 1), at_low), dict(q_up, gz=up_g)),
                (ref(pl.ds(first, 1), z_top), ref(pl.ds(last + 1, 1), at_low), dict(q_down, gz=up_g)),
                (ref(pl.ds(last, 1), z_low), ref(pl.ds(1, 1), at_top), dict(q_up, gz=down_g)),
                (ref(pl.ds(first, 1), z_low), ref(pl.ds(last + 1, 1), at_top), dict(q_down, gz=down_g)),
            )[slot]
            return pltpu.make_async_remote_copy(
                src_ref=frm, dst_ref=to, send_sem=halo_send.at[k, slot], recv_sem=halo_recv.at[k, slot],
                device_id=where, device_id_type=MESH)

        UP, DOWN, BOTH = (2, 4, 5), (3, 6, 7), (0, 1)

        def halo_start(k):
            @pl.when(has_up)
            def _():
                start_all([halo(k, s) for s in UP])

            @pl.when(has_down)
            def _():
                start_all([halo(k, s) for s in DOWN])

            start_all([halo(k, s) for s in BOTH])

        def halo_arrive(k):
            for s in BOTH:
                halo(k, s).wait_recv()

            @pl.when(has_down)
            def _():
                for s in UP:
                    halo(k, s).wait_recv()

            @pl.when(has_up)
            def _():
                for s in DOWN:
                    halo(k, s).wait_recv()

        def halo_sent(k):
            send_wait_all([halo(k, s) for s in BOTH])

            @pl.when(has_up)
            def _():
                send_wait_all([halo(k, s) for s in UP])

            @pl.when(has_down)
            def _():
                send_wait_all([halo(k, s) for s in DOWN])

        def swap(frm, to, slot):
            return pltpu.make_async_remote_copy(
                src_ref=frm, dst_ref=to, send_sem=halo_send.at[ITERS - 1, slot], recv_sem=halo_recv.at[ITERS - 1, slot],
                device_id={"row": sib}, device_id_type=MESH)

        other_lanes = pl.ds(pl.multiple_of(sib * s_r, s_r), s_r)
        own_rows = pl.ds(first, half)

        def total_wait(k):
            return pltpu.make_async_remote_copy(
                src_ref=G.at[k, pl.ds(1, peers - 1)], dst_ref=G.at[k, pl.ds(1, peers - 1)],
                send_sem=sum_sem.at[0, k], recv_sem=sum_sem.at[1, k], device_id={"row": sib}, device_id_type=MESH)

        for k in range(ITERS):
            cur = k % 2

            def perm_row(i, carry, k=k, cur=cur):
                a, b = A[i], B[i]
                here = Pot[cur, i]
                s0 = S[0, i] - 0.5 * (Pot[cur, i + 1] - Pot[cur, i - 1])
                s1 = S[1, i] - 0.5 * (z_up(here) - z_down(here))
                s2 = S[2, i] - 0.5 * (r_up(here, 0.0) - r_down(here, 0.0))
                field_sq = s0 * s0 + s1 * s1 + s2 * s2
                M[i] = 1.0 + a / (1.0 + field_sq * b)
                return carry

            if k > 0:
                lax.fori_loop(1, half + 3, perm_row, 0, unroll=True)

            def relax_row(i, carry, k=k, cur=cur):
                below, acc = carry
                m = M[i]
                mi = m[:s_z]
                above = conduct(mi, M[i + 1, :s_z])
                cz = conduct(m, z_up(m))
                cz_low = z_down(cz)[:s_z]
                cz = cz[:s_z]
                cr = conduct(mi, r_up(mi, 1.0))
                cr_low = conduct(mi, r_down(mi, 1.0))
                fz = m * S[1, i]
                fr = mi * S[2, i, :s_z]
                flux = M[i + 1, :s_z] * S[0, i + 1, :s_z] - M[i - 1, :s_z] * S[0, i - 1, :s_z]
                flux = flux + (z_up(fz) - z_down(fz))[:s_z] + (r_up(fr, 0.0) - r_down(fr, 0.0))
                numerator = -0.5 * flux
                if k > 0:
                    here = Pot[cur, i]
                    hi = here[:s_z]
                    numerator = (numerator + above * Pot[cur, i + 1, :s_z] + below * Pot[cur, i - 1, :s_z]
                                 + cz * z_up(here)[:s_z] + cz_low * z_down(here)[:s_z]
                                 + cr * r_up(hi, 0.0) + cr_low * r_down(hi, 0.0))
                relaxed = numerator / (above + below + cz + cz_low + cr + cr_low)
                if k == 0:
                    update = weights[0] * relaxed
                elif k == 1:
                    update = weights[1] * relaxed - hi
                else:
                    earlier = Pot[1 - cur, i, :s_z]
                    update = earlier + weights[k] * (relaxed - earlier) - hi
                U[k, i, :s_z] = update
                return above, acc + update * update

            start = conduct(M[1, :s_z], M[2, :s_z])
            _, acc = lax.fori_loop(first, last + 1, relax_row, (start, jnp.zeros((s_z, wide), jnp.float32)), unroll=True)

            acc = acc[:, :s_r] + acc[:, s_r:]
            part = acc[:8]
            for z in range(8, s_z, 8):
                part = part + acc[z : z + 8]
            G[k, 0:1] = jnp.sum(part, axis=0, keepdims=True)

            def share(j, where, k=k):
                pltpu.make_async_remote_copy(
                    src_ref=G.at[k, pl.ds(0, 1)], dst_ref=G.at[k, pl.ds(j, 1)], send_sem=sum_sem.at[0, k],
                    recv_sem=sum_sem.at[1, k], device_id=where, device_id_type=MESH).start()

            each_peer(share)
            if k < ITERS - 1:
                halo_start(k)
            else:
                give_update = swap(U.at[k, own_rows, whole_z, other_lanes], FU, 1)
                give_update.start()
            total_wait(k).wait_recv()
            sum_squares = jnp.sum(jnp.sum(G[k], axis=0, keepdims=True), axis=1, keepdims=True)
            factor = jnp.minimum(1.0, step_cap * lax.rsqrt(sum_squares * (1.0 / cell_count) + 1e-06))

            if k < ITERS - 1:
                halo_arrive(k)
                wide_factor = jnp.broadcast_to(factor, (tall, wide))

                def step(i, carry, k=k, cur=cur):
                    new = wide_factor * U[k, i]
                    if k > 0:
                        new = new + Pot[cur, i]
                    Pot[1 - cur, i] = new
                    return carry

                lax.fori_loop(0, half + 4, step, 0, unroll=True)
                if k == ITERS - 2:
                    give_potential = swap(Pot.at[1 - cur, own_rows, whole_z, other_lanes], FP, 0)
                    give_potential.start()
            else:
                wide_factor = jnp.broadcast_to(factor, (half, s_z, s_r))
                out[pl.ds(half * c, half)] = (
                    Pot[cur, first : last + 1, :s_z, lanes] + wide_factor * U[k, first : last + 1, :s_z, lanes])
                give_potential.wait_recv()
                give_update.wait_recv()
                out[pl.ds(half * sib, half)] = FP[...] + wide_factor * FU[...]

        send_wait_all(always)

        @pl.when(has_up)
        def _():
            send_wait_all(when_up)

        @pl.when(has_down)
        def _():
            send_wait_all(when_down)

        for k in range(ITERS):
            total_wait(k).wait_send()
            if k < ITERS - 1:
                halo_sent(k)
        give_potential.wait_send()
        give_update.wait_send()

    rows = half + 4
    scratch = [
        pltpu.VMEM((3, rows, tall, wide), jnp.float32),
        pltpu.VMEM((rows, tall, wide), jnp.int32),
        pltpu.VMEM((rows, tall, wide), jnp.float32),
        pltpu.VMEM((rows, tall, wide), jnp.float32),
        pltpu.VMEM((2, rows, tall, wide), jnp.float32),
        pltpu.VMEM((rows, tall, wide), jnp.float32),
        pltpu.VMEM((ITERS, rows, tall, wide), jnp.float32),
        pltpu.VMEM((ITERS, peers, s_r), jnp.float32),
        pltpu.VMEM((half, s_z, s_r), jnp.float32),
        pltpu.VMEM((half, s_z, s_r), jnp.float32),
        pltpu.VMEM((3,) + tuple(shape), jnp.float32),
        pltpu.VMEM(tuple(shape), jnp.int32),
        pltpu.SemaphoreType.DMA((2, ITERS)),
        pltpu.SemaphoreType.DMA((ITERS, 8)),
        pltpu.SemaphoreType.DMA((ITERS, 8)),
        pltpu.SemaphoreType.DMA((2, 7)),
        pltpu.SemaphoreType.DMA((2, 7)),
        pltpu.SemaphoreType.DMA((4,)),
    ]
    return pl.pallas_call(
        kernel,
        out_shape=jax.ShapeDtypeStruct(shape, jnp.float32),
        in_specs=[pl.BlockSpec(memory_space=pltpu.HBM)] * 2,
        out_specs=pl.BlockSpec(memory_space=pltpu.VMEM),
        scratch_shapes=scratch,
        compiler_params=pltpu.CompilerParams(
            collective_id=0, has_side_effects=True, vmem_limit_bytes=24 * 1024 * 1024),
        name="sweeps",
    )


def solution(mesh):
    sizes = mesh.shape

    def on_device(source_field, labels):
        return make_kernel(sizes["phi"], sizes["row"], sizes["gz"], labels.shape)(source_field, labels)

    placed = (P(None, ("group", "phi"), "gz", "row"), P(("group", "phi"), "gz", "row"))
    return jax.shard_map(
        on_device,
        mesh=mesh,
        in_specs=placed,
        out_specs=P(("group", "phi"), "gz", "row"),
        check_vma=False,
    )
```

```python
import jax
import jax.numpy as jnp
from jax import lax
from jax.experimental import pallas as pl
from jax.experimental.pallas import tpu as pltpu
from jax.sharding import PartitionSpec as P

ITERS = 4
iron_perm = 40.0
iron_sat = 0.25
coil_perm = 4.0
coil_sat = 1.0
step_cap = 0.1
spectral = 0.9
MESH = pl.DeviceIdType.MESH


def chebyshev_weights(sweep_count):
    weights = [1.0]
    weights.append(1.0 / (1.0 - spectral * spectral / 2.0))
    while len(weights) < sweep_count:
        weights.append(1.0 / (1.0 - spectral * spectral * weights[-1] / 4.0))
    return weights


def make_kernel(n_phi, n_row, n_gz, shape):
    s_phi, s_z, s_r = shape
    peers = n_phi * n_row * n_gz
    half = s_phi // 2
    wide = 2 * s_r
    tall = s_z + 8
    cell_count = s_phi * s_z * s_r * peers
    weights = chebyshev_weights(ITERS)
    first, last = 2, half + 1

    def kernel(src, lab, out, S, L, A, B, Pot, M, U, G, FP, FU, X, XL, sum_sem, halo_send, halo_recv, in_send, in_recv, loc_sem):
        p = lax.axis_index("phi")
        c = lax.axis_index("row")
        g = lax.axis_index("gz")
        lanes = pl.ds(pl.multiple_of(c * s_r, s_r), s_r)
        sib = 1 - c

        def own_part(core):
            return pl.ds((half - 1) * core, half + 1), pl.ds(2 - core, half + 1)

        def cut(ref, rows, z):
            return ref.at[:, rows, z, :] if ref is src or ref is X else ref.at[rows, z, :]

        def land(ref, rows, z):
            return ref.at[:, rows, z, lanes] if ref is S else ref.at[rows, z, lanes]

        whole_z = pl.ds(0, s_z)
        local, stages = [], []
        for n, (a, b, staged) in enumerate(((src, S, X), (lab, L, XL))):
            stage = pltpu.make_async_copy(a, staged, loc_sem.at[2 + n])
            stage.start()
            stages.append(stage)
            frm, to = own_part(c)
            copy = pltpu.make_async_copy(cut(a, frm, whole_z), land(b, to, whole_z), loc_sem.at[n])
            copy.start()
            local.append(copy)

        def along_phi(d):
            if n_phi == 4 and peers <= 32:
                return (p, p + 1 - 2 * lax.rem(p, 2), lax.rem(p + 2, 4), 3 - p)[d]
            return lax.rem(p + d, n_phi)

        def peer(j):
            return {
                "phi": along_phi(j // (n_row * n_gz)),
                "row": lax.rem(c + (j // n_gz) % n_row, n_row),
                "gz": lax.rem(g + j % n_gz, n_gz),
            }

        def each_peer(body):
            if peers > 32:
                lax.fori_loop(1, peers, lambda j, carry: (body(j, peer(j)), carry)[1], 0)
            else:
                for j, where in peer_list:
                    body(j, where)

        if peers <= 32:
            per_chip = n_row * n_gz
            order = sorted(range(1, peers), key=lambda j: (-(j // per_chip), -(j % n_gz)))
            peer_list = [(j, peer(j)) for j in order]

        rim = pl.ds(s_z, 8)
        S[:, :, rim, :] = jnp.zeros((3, half + 4, 8, wide), jnp.float32)
        L[:, rim, :] = jnp.zeros((half + 4, 8, wide), jnp.int32)
        for k in range(ITERS - 1):
            U[k, :, rim, :] = jnp.zeros((half + 4, 8, wide), jnp.float32)

        barrier = pltpu.get_barrier_semaphore()

        def greet(j, where):
            pl.semaphore_signal(barrier, inc=1, device_id=where, device_id_type=MESH)

        each_peer(greet)
        pl.semaphore_wait(barrier, peers - 1)

        for stage in stages:
            stage.wait()
        up_p, down_p = lax.rem(p + 1, n_phi), lax.rem(p + n_phi - 1, n_phi)
        has_up, has_down = g < n_gz - 1, g > 0
        up_g, down_g = jnp.minimum(g + 1, n_gz - 1), jnp.maximum(g - 1, 0)

        always, when_up, when_down = [], [], []
        for n, (a, b) in enumerate(((X, S), (XL, L))):
            def remote(frm, to, send, recv, where, n=n):
                return pltpu.make_async_remote_copy(
                    src_ref=frm, dst_ref=to, send_sem=in_send.at[n, send], recv_sem=in_recv.at[n, recv],
                    device_id=where, device_id_type=MESH)

            frm, to = own_part(sib)
            always.append(remote(cut(a, pl.ds(s_phi - 1, 1), whole_z), land(b, pl.ds(1, 1), whole_z), 1, 1 + c,
                                 {"phi": up_p, "row": 0}))
            always.append(remote(cut(a, pl.ds(0, 1), whole_z), land(b, pl.ds(last + 1, 1), whole_z), 2, 1 + c,
                                 {"phi": down_p, "row": 1}))
            always.append(remote(cut(a, frm, whole_z), land(b, to, whole_z), 0, 0, {"row": sib}))
            for t in range(2):
                rows = pl.ds(half * t, half)
                when_up.append(remote(cut(a, rows, pl.ds(s_z - 1, 1)), land(b, pl.ds(first, half), pl.ds(tall - 1, 1)),
                                      3 + t, 3 + c, {"gz": up_g, "row": t}))
                when_down.append(remote(cut(a, rows, pl.ds(0, 1)), land(b, pl.ds(first, half), pl.ds(s_z, 1)),
                                        5 + t, 5 + c, {"gz": down_g, "row": t}))

        def start_all(copies):
            for copy in copies:
                copy.start()

        def send_wait_all(copies):
            for copy in copies:
                copy.wait_send()

        start_all(always)

        @pl.when(has_up)
        def _():
            start_all(when_up)

        @pl.when(has_down)
        def _():
            start_all(when_down)

        def arrived(b, n, slot, rows, z, ln):
            ref = b.at[:, rows, z, ln] if b is S else b.at[rows, z, ln]
            pltpu.make_async_remote_copy(
                src_ref=ref, dst_ref=ref, send_sem=in_send.at[n, 0], recv_sem=in_recv.at[n, slot],
                device_id={"row": sib}, device_id_type=MESH).wait_recv()

        def first_perm(i, z):
            label = L[i, z]
            a = jnp.where(label == 1, iron_perm - 1.0, jnp.where(label == 2, coil_perm - 1.0, 0.0))
            b = jnp.where(label == 1, 1.0 / iron_sat, jnp.where(label == 2, 1.0 / coil_sat, 0.0))
            A[i, z] = a
            B[i, z] = b
            s0, s1, s2 = S[0, i, z], S[1, i, z], S[2, i, z]
            M[i, z] = 1.0 + a / (1.0 + (s0 * s0 + s1 * s1 + s2 * s2) * b)

        for copy in local:
            copy.wait()
        for n, b in enumerate((S, L)):
            arrived(b, n, 0, own_part(c)[1], whole_z, pl.ds(pl.multiple_of(sib * s_r, s_r), s_r))
        for i in range(first, last + 1):
            first_perm(i, whole_z)
        near = jnp.where(c == 0, last + 1, 1)
        first_perm(near, whole_z)
        for n, b in enumerate((S, L)):
            for core in range(2):
                arrived(b, n, 1 + core, pl.ds(jnp.where(c == 0, 1, last + 1), 1), whole_z, pl.ds(core * s_r, s_r))
        first_perm(last + 2 - near, whole_z)

        @pl.when(has_down)
        def _():
            for n, b in enumerate((S, L)):
                for core in range(2):
                    arrived(b, n, 3 + core, pl.ds(first, half), pl.ds(tall - 1, 1), pl.ds(core * s_r, s_r))

        @pl.when(has_up)
        def _():
            for n, b in enumerate((S, L)):
                for core in range(2):
                    arrived(b, n, 5 + core, pl.ds(first, half), pl.ds(s_z, 1), pl.ds(core * s_r, s_r))

        for i in range(1, last + 2):
            first_perm(i, rim)

        lane = lax.broadcasted_iota(jnp.int32, (tall, wide), 1)
        at_end, at_start = lane == wide - 1, lane == 0

        def z_up(x):
            return pltpu.roll(x, tall - 1, 0)

        def z_down(x):
            return pltpu.roll(x, 1, 0)

        def r_up(x, edge):
            return jnp.where(at_end[: x.shape[0]], edge, pltpu.roll(x, wide - 1, 1))

        def r_down(x, edge):
            return jnp.where(at_start[: x.shape[0]], edge, pltpu.roll(x, 1, 1))

        def conduct(a, b):
            return 2.0 * a * b / (a + b)

        q_up = {"phi": jnp.where(c == 1, up_p, p), "row": sib}
        q_down = {"phi": jnp.where(c == 0, down_p, p), "row": sib}
        z_top, z_low = pl.ds(s_z - 2, 2), pl.ds(0, 2)
        at_low, at_top = pl.ds(tall - 2, 2), pl.ds(s_z, 2)

        def halo(k, slot):
            def ref(rows, z):
                return U.at[k, rows, z, :]

            own = pl.ds(first, half)
            frm, to, where = (
                (ref(pl.ds(last - 1, 2), whole_z), ref(pl.ds(0, 2), whole_z), q_up),
                (ref(pl.ds(first, 2), whole_z), ref(pl.ds(last + 1, 2), whole_z), q_down),
                (ref(own, z_top), ref(own, at_low), {"gz": up_g}),
                (ref(own, z_low), ref(own, at_top), {"gz": down_g}),
                (ref(pl.ds(last, 1), z_top), ref(pl.ds(1, 1), at_low), dict(q_up, gz=up_g)),
                (ref(pl.ds(first, 1), z_top), ref(pl.ds(last + 1, 1), at_low), dict(q_down, gz=up_g)),
                (ref(pl.ds(last, 1), z_low), ref(pl.ds(1, 1), at_top), dict(q_up, gz=down_g)),
                (ref(pl.ds(first, 1), z_low), ref(pl.ds(last + 1, 1), at_top), dict(q_down, gz=down_g)),
            )[slot]
            return pltpu.make_async_remote_copy(
                src_ref=frm, dst_ref=to, send_sem=halo_send.at[k, slot], recv_sem=halo_recv.at[k, slot],
                device_id=where, device_id_type=MESH)

        UP, DOWN, BOTH = (2, 4, 5), (3, 6, 7), (0, 1)

        def halo_start(k):
            @pl.when(has_up)
            def _():
                start_all([halo(k, s) for s in UP])

            @pl.when(has_down)
            def _():
                start_all([halo(k, s) for s in DOWN])

            start_all([halo(k, s) for s in BOTH])

        def halo_arrive(k):
            for s in BOTH:
                halo(k, s).wait_recv()

            @pl.when(has_down)
            def _():
                for s in UP:
                    halo(k, s).wait_recv()

            @pl.when(has_up)
            def _():
                for s in DOWN:
                    halo(k, s).wait_recv()

        def halo_sent(k):
            send_wait_all([halo(k, s) for s in BOTH])

            @pl.when(has_up)
            def _():
                send_wait_all([halo(k, s) for s in UP])

            @pl.when(has_down)
            def _():
                send_wait_all([halo(k, s) for s in DOWN])

        def swap(frm, to, slot):
            return pltpu.make_async_remote_copy(
                src_ref=frm, dst_ref=to, send_sem=halo_send.at[ITERS - 1, slot], recv_sem=halo_recv.at[ITERS - 1, slot],
                device_id={"row": sib}, device_id_type=MESH)

        other_lanes = pl.ds(pl.multiple_of(sib * s_r, s_r), s_r)
        own_rows = pl.ds(first, half)

        def total_wait(k):
            return pltpu.make_async_remote_copy(
                src_ref=G.at[k, pl.ds(1, peers - 1)], dst_ref=G.at[k, pl.ds(1, peers - 1)],
                send_sem=sum_sem.at[0, k], recv_sem=sum_sem.at[1, k], device_id={"row": sib}, device_id_type=MESH)

        for k in range(ITERS):
            cur = k % 2

            def perm_row(i, carry, k=k, cur=cur):
                a, b = A[i], B[i]
                here = Pot[cur, i]
                s0 = S[0, i] - 0.5 * (Pot[cur, i + 1] - Pot[cur, i - 1])
                s1 = S[1, i] - 0.5 * (z_up(here) - z_down(here))
                s2 = S[2, i] - 0.5 * (r_up(here, 0.0) - r_down(here, 0.0))
                field_sq = s0 * s0 + s1 * s1 + s2 * s2
                M[i] = 1.0 + a / (1.0 + field_sq * b)
                return carry

            if k > 0:
                lax.fori_loop(1, half + 3, perm_row, 0, unroll=True)

            def relax_row(i, carry, k=k, cur=cur):
                below, acc = carry
                m = M[i]
                mi = m[:s_z]
                above = conduct(mi, M[i + 1, :s_z])
                cz = conduct(m, z_up(m))
                cz_low = z_down(cz)[:s_z]
                cz = cz[:s_z]
                cr = conduct(mi, r_up(mi, 1.0))
                cr_low = conduct(mi, r_down(mi, 1.0))
                fz = m * S[1, i]
                fr = mi * S[2, i, :s_z]
                flux = M[i + 1, :s_z] * S[0, i + 1, :s_z] - M[i - 1, :s_z] * S[0, i - 1, :s_z]
                flux = flux + (z_up(fz) - z_down(fz))[:s_z] + (r_up(fr, 0.0) - r_down(fr, 0.0))
                numerator = -0.5 * flux
                if k > 0:
                    here = Pot[cur, i]
                    hi = here[:s_z]
                    numerator = (numerator + above * Pot[cur, i + 1, :s_z] + below * Pot[cur, i - 1, :s_z]
                                 + cz * z_up(here)[:s_z] + cz_low * z_down(here)[:s_z]
                                 + cr * r_up(hi, 0.0) + cr_low * r_down(hi, 0.0))
                relaxed = numerator / (above + below + cz + cz_low + cr + cr_low)
                if k == 0:
                    update = weights[0] * relaxed
                elif k == 1:
                    update = weights[1] * relaxed - hi
                else:
                    earlier = Pot[1 - cur, i, :s_z]
                    update = earlier + weights[k] * (relaxed - earlier) - hi
                U[k, i, :s_z] = update
                return above, acc + update * update

            start = conduct(M[1, :s_z], M[2, :s_z])
            _, acc = lax.fori_loop(first, last + 1, relax_row, (start, jnp.zeros((s_z, wide), jnp.float32)), unroll=True)

            acc = acc[:, :s_r] + acc[:, s_r:]
            part = acc[:8]
            for z in range(8, s_z, 8):
                part = part + acc[z : z + 8]
            G[k, 0:1] = jnp.sum(part, axis=0, keepdims=True)

            def share(j, where, k=k):
                pltpu.make_async_remote_copy(
                    src_ref=G.at[k, pl.ds(0, 1)], dst_ref=G.at[k, pl.ds(j, 1)], send_sem=sum_sem.at[0, k],
                    recv_sem=sum_sem.at[1, k], device_id=where, device_id_type=MESH).start()

            each_peer(share)
            if k < ITERS - 1:
                halo_start(k)
            else:
                give_update = swap(U.at[k, own_rows, whole_z, other_lanes], FU, 1)
                give_update.start()
            total_wait(k).wait_recv()
            sum_squares = jnp.sum(jnp.sum(G[k], axis=0, keepdims=True), axis=1, keepdims=True)
            factor = jnp.minimum(1.0, step_cap * lax.rsqrt(sum_squares * (1.0 / cell_count) + 1e-06))

            if k < ITERS - 1:
                halo_arrive(k)
                wide_factor = jnp.broadcast_to(factor, (tall, wide))

                def step(i, carry, k=k, cur=cur):
                    new = wide_factor * U[k, i]
                    if k > 0:
                        new = new + Pot[cur, i]
                    Pot[1 - cur, i] = new
                    return carry

                lax.fori_loop(0, half + 4, step, 0, unroll=True)
                if k == ITERS - 2:
                    give_potential = swap(Pot.at[1 - cur, own_rows, whole_z, other_lanes], FP, 0)
                    give_potential.start()
            else:
                wide_factor = jnp.broadcast_to(factor, (half, s_z, s_r))
                out[pl.ds(half * c, half)] = (
                    Pot[cur, first : last + 1, :s_z, lanes] + wide_factor * U[k, first : last + 1, :s_z, lanes])
                give_potential.wait_recv()
                give_update.wait_recv()
                out[pl.ds(half * sib, half)] = FP[...] + wide_factor * FU[...]

        send_wait_all(always)

        @pl.when(has_up)
        def _():
            send_wait_all(when_up)

        @pl.when(has_down)
        def _():
            send_wait_all(when_down)

        for k in range(ITERS):
            total_wait(k).wait_send()
            if k < ITERS - 1:
                halo_sent(k)
        give_potential.wait_send()
        give_update.wait_send()

    rows = half + 4
    scratch = [
        pltpu.VMEM((3, rows, tall, wide), jnp.float32),
        pltpu.VMEM((rows, tall, wide), jnp.int32),
        pltpu.VMEM((rows, tall, wide), jnp.float32),
        pltpu.VMEM((rows, tall, wide), jnp.float32),
        pltpu.VMEM((2, rows, tall, wide), jnp.float32),
        pltpu.VMEM((rows, tall, wide), jnp.float32),
        pltpu.VMEM((ITERS, rows, tall, wide), jnp.float32),
        pltpu.VMEM((ITERS, peers, s_r), jnp.float32),
        pltpu.VMEM((half, s_z, s_r), jnp.float32),
        pltpu.VMEM((half, s_z, s_r), jnp.float32),
        pltpu.VMEM((3,) + tuple(shape), jnp.float32),
        pltpu.VMEM(tuple(shape), jnp.int32),
        pltpu.SemaphoreType.DMA((2, ITERS)),
        pltpu.SemaphoreType.DMA((ITERS, 8)),
        pltpu.SemaphoreType.DMA((ITERS, 8)),
        pltpu.SemaphoreType.DMA((2, 7)),
        pltpu.SemaphoreType.DMA((2, 7)),
        pltpu.SemaphoreType.DMA((4,)),
    ]
    return pl.pallas_call(
        kernel,
        out_shape=jax.ShapeDtypeStruct(shape, jnp.float32),
        in_specs=[pl.BlockSpec(memory_space=pltpu.HBM)] * 2,
        out_specs=pl.BlockSpec(memory_space=pltpu.VMEM),
        scratch_shapes=scratch,
        compiler_params=pltpu.CompilerParams(
            collective_id=0, has_side_effects=True, vmem_limit_bytes=24 * 1024 * 1024),
        name="sweeps",
    )


def solution(mesh):
    sizes = mesh.shape

    def on_device(source_field, labels):
        return make_kernel(sizes["phi"], sizes["row"], sizes["gz"], labels.shape)(source_field, labels)

    placed = (P(None, ("group", "phi"), "gz", "row"), P(("group", "phi"), "gz", "row"))
    return jax.shard_map(
        on_device,
        mesh=mesh,
        in_specs=placed,
        out_specs=P(("group", "phi"), "gz", "row"),
        check_vma=False,
    )
```

```python
import jax
import jax.numpy as jnp
from jax import lax
from jax.experimental import pallas as pl
from jax.experimental.pallas import tpu as pltpu
from jax.sharding import PartitionSpec as P

ITERS = 4
iron_perm = 40.0
iron_sat = 0.25
coil_perm = 4.0
coil_sat = 1.0
step_cap = 0.1
spectral = 0.9
MESH = pl.DeviceIdType.MESH


def chebyshev_weights(sweep_count):
    weights = [1.0]
    weights.append(1.0 / (1.0 - spectral * spectral / 2.0))
    while len(weights) < sweep_count:
        weights.append(1.0 / (1.0 - spectral * spectral * weights[-1] / 4.0))
    return weights


def make_kernel(n_phi, n_row, n_gz, shape):
    s_phi, s_z, s_r = shape
    peers = n_phi * n_row * n_gz
    half = s_phi // 2
    wide = 2 * s_r
    tall = s_z + 8
    cell_count = s_phi * s_z * s_r * peers
    weights = chebyshev_weights(ITERS)
    first, last = 2, half + 1

    def kernel(src, lab, out, S, L, A, B, Pot, M, U, G, FP, FU, X, XL, sum_sem, halo_send, halo_recv, in_send, in_recv, loc_sem):
        p = lax.axis_index("phi")
        c = lax.axis_index("row")
        g = lax.axis_index("gz")
        lanes = pl.ds(pl.multiple_of(c * s_r, s_r), s_r)
        sib = 1 - c

        def own_part(core):
            return pl.ds((half - 1) * core, half + 1), pl.ds(2 - core, half + 1)

        def cut(ref, rows, z):
            return ref.at[:, rows, z, :] if ref is src or ref is X else ref.at[rows, z, :]

        def land(ref, rows, z):
            return ref.at[:, rows, z, lanes] if ref is S else ref.at[rows, z, lanes]

        whole_z = pl.ds(0, s_z)
        local, stages = [], []
        for n, (a, b, staged) in enumerate(((src, S, X), (lab, L, XL))):
            stage = pltpu.make_async_copy(a, staged, loc_sem.at[2 + n])
            stage.start()
            stages.append(stage)
            frm, to = own_part(c)
            copy = pltpu.make_async_copy(cut(a, frm, whole_z), land(b, to, whole_z), loc_sem.at[n])
            copy.start()
            local.append(copy)

        def along_phi(d):
            if n_phi == 4 and peers <= 32:
                return (p, p + 1 - 2 * lax.rem(p, 2), lax.rem(p + 2, 4), 3 - p)[d]
            return lax.rem(p + d, n_phi)

        def peer(j):
            return {
                "phi": along_phi(j // (n_row * n_gz)),
                "row": lax.rem(c + (j // n_gz) % n_row, n_row),
                "gz": lax.rem(g + j % n_gz, n_gz),
            }

        def each_peer(body):
            if peers > 32:
                lax.fori_loop(1, peers, lambda j, carry: (body(j, peer(j)), carry)[1], 0)
            else:
                for j, where in peer_list:
                    body(j, where)

        if peers <= 32:
            per_chip = n_row * n_gz
            order = sorted(range(1, peers), key=lambda j: (-(j // per_chip), -(j % n_gz)))
            peer_list = [(j, peer(j)) for j in order]

        rim = pl.ds(s_z, 8)
        S[:, :, rim, :] = jnp.zeros((3, half + 4, 8, wide), jnp.float32)
        L[:, rim, :] = jnp.zeros((half + 4, 8, wide), jnp.int32)
        for k in range(ITERS - 1):
            U[k, :, rim, :] = jnp.zeros((half + 4, 8, wide), jnp.float32)

        barrier = pltpu.get_barrier_semaphore()

        def greet(j, where):
            pl.semaphore_signal(barrier, inc=1, device_id=where, device_id_type=MESH)

        each_peer(greet)
        pl.semaphore_wait(barrier, peers - 1)

        for stage in stages:
            stage.wait()
        up_p, down_p = lax.rem(p + 1, n_phi), lax.rem(p + n_phi - 1, n_phi)
        has_up, has_down = g < n_gz - 1, g > 0
        up_g, down_g = jnp.minimum(g + 1, n_gz - 1), jnp.maximum(g - 1, 0)

        always, when_up, when_down = [], [], []
        for n, (a, b) in enumerate(((X, S), (XL, L))):
            def remote(frm, to, send, recv, where, n=n):
                return pltpu.make_async_remote_copy(
                    src_ref=frm, dst_ref=to, send_sem=in_send.at[n, send], recv_sem=in_recv.at[n, recv],
                    device_id=where, device_id_type=MESH)

            frm, to = own_part(sib)
            always.append(remote(cut(a, pl.ds(s_phi - 1, 1), whole_z), land(b, pl.ds(1, 1), whole_z), 1, 1 + c,
                                 {"phi": up_p, "row": 0}))
            always.append(remote(cut(a, pl.ds(0, 1), whole_z), land(b, pl.ds(last + 1, 1), whole_z), 2, 1 + c,
                                 {"phi": down_p, "row": 1}))
            always.append(remote(cut(a, frm, whole_z), land(b, to, whole_z), 0, 0, {"row": sib}))
            for t in range(2):
                rows = pl.ds(half * t, half)
                when_up.append(remote(cut(a, rows, pl.ds(s_z - 1, 1)), land(b, pl.ds(first, half), pl.ds(tall - 1, 1)),
                                      3 + t, 3 + c, {"gz": up_g, "row": t}))
                when_down.append(remote(cut(a, rows, pl.ds(0, 1)), land(b, pl.ds(first, half), pl.ds(s_z, 1)),
                                        5 + t, 5 + c, {"gz": down_g, "row": t}))

        def start_all(copies):
            for copy in copies:
                copy.start()

        def send_wait_all(copies):
            for copy in copies:
                copy.wait_send()

        start_all(always)

        @pl.when(has_up)
        def _():
            start_all(when_up)

        @pl.when(has_down)
        def _():
            start_all(when_down)

        def arrived(b, n, slot, rows, z, ln):
            ref = b.at[:, rows, z, ln] if b is S else b.at[rows, z, ln]
            pltpu.make_async_remote_copy(
                src_ref=ref, dst_ref=ref, send_sem=in_send.at[n, 0], recv_sem=in_recv.at[n, slot],
                device_id={"row": sib}, device_id_type=MESH).wait_recv()

        def first_perm(i, z):
            label = L[i, z]
            a = jnp.where(label == 1, iron_perm - 1.0, jnp.where(label == 2, coil_perm - 1.0, 0.0))
            b = jnp.where(label == 1, 1.0 / iron_sat, jnp.where(label == 2, 1.0 / coil_sat, 0.0))
            A[i, z] = a
            B[i, z] = b
            s0, s1, s2 = S[0, i, z], S[1, i, z], S[2, i, z]
            M[i, z] = 1.0 + a / (1.0 + (s0 * s0 + s1 * s1 + s2 * s2) * b)

        for copy in local:
            copy.wait()
        for n, b in enumerate((S, L)):
            arrived(b, n, 0, own_part(c)[1], whole_z, pl.ds(pl.multiple_of(sib * s_r, s_r), s_r))
        for i in range(first, last + 1):
            first_perm(i, whole_z)
        near = jnp.where(c == 0, last + 1, 1)
        first_perm(near, whole_z)
        for n, b in enumerate((S, L)):
            for core in range(2):
                arrived(b, n, 1 + core, pl.ds(jnp.where(c == 0, 1, last + 1), 1), whole_z, pl.ds(core * s_r, s_r))
        first_perm(last + 2 - near, whole_z)

        @pl.when(has_down)
        def _():
            for n, b in enumerate((S, L)):
                for core in range(2):
                    arrived(b, n, 3 + core, pl.ds(first, half), pl.ds(tall - 1, 1), pl.ds(core * s_r, s_r))

        @pl.when(has_up)
        def _():
            for n, b in enumerate((S, L)):
                for core in range(2):
                    arrived(b, n, 5 + core, pl.ds(first, half), pl.ds(s_z, 1), pl.ds(core * s_r, s_r))

        for i in range(1, last + 2):
            first_perm(i, rim)

        lane = lax.broadcasted_iota(jnp.int32, (tall, wide), 1)
        at_end, at_start = lane == wide - 1, lane == 0

        def z_up(x):
            return pltpu.roll(x, tall - 1, 0)

        def z_down(x):
            return pltpu.roll(x, 1, 0)

        def r_up(x, edge):
            return jnp.where(at_end[: x.shape[0]], edge, pltpu.roll(x, wide - 1, 1))

        def r_down(x, edge):
            return jnp.where(at_start[: x.shape[0]], edge, pltpu.roll(x, 1, 1))

        def conduct(a, b):
            return 2.0 * a * b / (a + b)

        q_up = {"phi": jnp.where(c == 1, up_p, p), "row": sib}
        q_down = {"phi": jnp.where(c == 0, down_p, p), "row": sib}
        z_top, z_low = pl.ds(s_z - 2, 2), pl.ds(0, 2)
        at_low, at_top = pl.ds(tall - 2, 2), pl.ds(s_z, 2)

        def halo(k, slot):
            def ref(rows, z):
                return U.at[k, rows, z, :]

            own = pl.ds(first, half)
            frm, to, where = (
                (ref(pl.ds(last - 1, 2), whole_z), ref(pl.ds(0, 2), whole_z), q_up),
                (ref(pl.ds(first, 2), whole_z), ref(pl.ds(last + 1, 2), whole_z), q_down),
                (ref(own, z_top), ref(own, at_low), {"gz": up_g}),
                (ref(own, z_low), ref(own, at_top), {"gz": down_g}),
                (ref(pl.ds(last, 1), z_top), ref(pl.ds(1, 1), at_low), dict(q_up, gz=up_g)),
                (ref(pl.ds(first, 1), z_top), ref(pl.ds(last + 1, 1), at_low), dict(q_down, gz=up_g)),
                (ref(pl.ds(last, 1), z_low), ref(pl.ds(1, 1), at_top), dict(q_up, gz=down_g)),
                (ref(pl.ds(first, 1), z_low), ref(pl.ds(last + 1, 1), at_top), dict(q_down, gz=down_g)),
            )[slot]
            return pltpu.make_async_remote_copy(
                src_ref=frm, dst_ref=to, send_sem=halo_send.at[k, slot], recv_sem=halo_recv.at[k, slot],
                device_id=where, device_id_type=MESH)

        UP, DOWN, BOTH = (2, 4, 5), (3, 6, 7), (0, 1)

        def halo_start(k):
            start_all([halo(k, s) for s in BOTH])

            @pl.when(has_up)
            def _():
                start_all([halo(k, s) for s in UP])

            @pl.when(has_down)
            def _():
                start_all([halo(k, s) for s in DOWN])

        def halo_arrive(k):
            for s in BOTH:
                halo(k, s).wait_recv()

            @pl.when(has_down)
            def _():
                for s in UP:
                    halo(k, s).wait_recv()

            @pl.when(has_up)
            def _():
                for s in DOWN:
                    halo(k, s).wait_recv()

        def halo_sent(k):
            send_wait_all([halo(k, s) for s in BOTH])

            @pl.when(has_up)
            def _():
                send_wait_all([halo(k, s) for s in UP])

            @pl.when(has_down)
            def _():
                send_wait_all([halo(k, s) for s in DOWN])

        def swap(frm, to, slot):
            return pltpu.make_async_remote_copy(
                src_ref=frm, dst_ref=to, send_sem=halo_send.at[ITERS - 1, slot], recv_sem=halo_recv.at[ITERS - 1, slot],
                device_id={"row": sib}, device_id_type=MESH)

        other_lanes = pl.ds(pl.multiple_of(sib * s_r, s_r), s_r)
        own_rows = pl.ds(first, half)

        def total_wait(k):
            return pltpu.make_async_remote_copy(
                src_ref=G.at[k, pl.ds(1, peers - 1)], dst_ref=G.at[k, pl.ds(1, peers - 1)],
                send_sem=sum_sem.at[0, k], recv_sem=sum_sem.at[1, k], device_id={"row": sib}, device_id_type=MESH)

        for k in range(ITERS):
            cur = k % 2

            def perm_row(i, carry, k=k, cur=cur):
                a, b = A[i], B[i]
                here = Pot[cur, i]
                s0 = S[0, i] - 0.5 * (Pot[cur, i + 1] - Pot[cur, i - 1])
                s1 = S[1, i] - 0.5 * (z_up(here) - z_down(here))
                s2 = S[2, i] - 0.5 * (r_up(here, 0.0) - r_down(here, 0.0))
                field_sq = s0 * s0 + s1 * s1 + s2 * s2
                M[i] = 1.0 + a / (1.0 + field_sq * b)
                return carry

            if k > 0:
                lax.fori_loop(1, half + 3, perm_row, 0, unroll=True)

            def relax_row(i, carry, k=k, cur=cur):
                below, acc = carry
                m = M[i]
                mi = m[:s_z]
                above = conduct(mi, M[i + 1, :s_z])
                cz = conduct(m, z_up(m))
                cz_low = z_down(cz)[:s_z]
                cz = cz[:s_z]
                cr = conduct(mi, r_up(mi, 1.0))
                cr_low = jnp.where(at_start[:s_z], 2.0 * mi / (mi + 1.0), pltpu.roll(cr, 1, 1))
                fz = m * S[1, i]
                fr = mi * S[2, i, :s_z]
                flux = M[i + 1, :s_z] * S[0, i + 1, :s_z] - M[i - 1, :s_z] * S[0, i - 1, :s_z]
                flux = flux + (z_up(fz) - z_down(fz))[:s_z] + (r_up(fr, 0.0) - r_down(fr, 0.0))
                numerator = -0.5 * flux
                if k > 0:
                    here = Pot[cur, i]
                    hi = here[:s_z]
                    numerator = (numerator + above * Pot[cur, i + 1, :s_z] + below * Pot[cur, i - 1, :s_z]
                                 + cz * z_up(here)[:s_z] + cz_low * z_down(here)[:s_z]
                                 + cr * r_up(hi, 0.0) + cr_low * r_down(hi, 0.0))
                relaxed = numerator / (above + below + cz + cz_low + cr + cr_low)
                if k == 0:
                    update = weights[0] * relaxed
                elif k == 1:
                    update = weights[1] * relaxed - hi
                else:
                    earlier = Pot[1 - cur, i, :s_z]
                    update = earlier + weights[k] * (relaxed - earlier) - hi
                U[k, i, :s_z] = update
                return above, acc + update * update

            start = conduct(M[1, :s_z], M[2, :s_z])
            _, acc = lax.fori_loop(first, last + 1, relax_row, (start, jnp.zeros((s_z, wide), jnp.float32)), unroll=True)

            acc = acc[:, :s_r] + acc[:, s_r:]
            part = acc[:8]
            for z in range(8, s_z, 8):
                part = part + acc[z : z + 8]
            G[k, 0:1] = jnp.sum(part, axis=0, keepdims=True)

            def share(j, where, k=k):
                pltpu.make_async_remote_copy(
                    src_ref=G.at[k, pl.ds(0, 1)], dst_ref=G.at[k, pl.ds(j, 1)], send_sem=sum_sem.at[0, k],
                    recv_sem=sum_sem.at[1, k], device_id=where, device_id_type=MESH).start()

            each_peer(share)
            if k < ITERS - 1:
                halo_start(k)
            else:
                give_update = swap(U.at[k, own_rows, whole_z, other_lanes], FU, 1)
                give_update.start()
            total_wait(k).wait_recv()
            sum_squares = jnp.sum(jnp.sum(G[k], axis=0, keepdims=True), axis=1, keepdims=True)
            factor = jnp.minimum(1.0, step_cap * lax.rsqrt(sum_squares * (1.0 / cell_count) + 1e-06))

            if k < ITERS - 1:
                halo_arrive(k)
                wide_factor = jnp.broadcast_to(factor, (tall, wide))

                def step(i, carry, k=k, cur=cur):
                    new = wide_factor * U[k, i]
                    if k > 0:
                        new = new + Pot[cur, i]
                    Pot[1 - cur, i] = new
                    return carry

                lax.fori_loop(0, half + 4, step, 0, unroll=True)
                if k == ITERS - 2:
                    give_potential = swap(Pot.at[1 - cur, own_rows, whole_z, other_lanes], FP, 0)
                    give_potential.start()
            else:
                wide_factor = jnp.broadcast_to(factor, (half, s_z, s_r))
                out[pl.ds(half * c, half)] = (
                    Pot[cur, first : last + 1, :s_z, lanes] + wide_factor * U[k, first : last + 1, :s_z, lanes])
                give_potential.wait_recv()
                give_update.wait_recv()
                out[pl.ds(half * sib, half)] = FP[...] + wide_factor * FU[...]

        send_wait_all(always)

        @pl.when(has_up)
        def _():
            send_wait_all(when_up)

        @pl.when(has_down)
        def _():
            send_wait_all(when_down)

        for k in range(ITERS):
            total_wait(k).wait_send()
            if k < ITERS - 1:
                halo_sent(k)
        give_potential.wait_send()
        give_update.wait_send()

    rows = half + 4
    scratch = [
        pltpu.VMEM((3, rows, tall, wide), jnp.float32),
        pltpu.VMEM((rows, tall, wide), jnp.int32),
        pltpu.VMEM((rows, tall, wide), jnp.float32),
        pltpu.VMEM((rows, tall, wide), jnp.float32),
        pltpu.VMEM((2, rows, tall, wide), jnp.float32),
        pltpu.VMEM((rows, tall, wide), jnp.float32),
        pltpu.VMEM((ITERS, rows, tall, wide), jnp.float32),
        pltpu.VMEM((ITERS, peers, s_r), jnp.float32),
        pltpu.VMEM((half, s_z, s_r), jnp.float32),
        pltpu.VMEM((half, s_z, s_r), jnp.float32),
        pltpu.VMEM((3,) + tuple(shape), jnp.float32),
        pltpu.VMEM(tuple(shape), jnp.int32),
        pltpu.SemaphoreType.DMA((2, ITERS)),
        pltpu.SemaphoreType.DMA((ITERS, 8)),
        pltpu.SemaphoreType.DMA((ITERS, 8)),
        pltpu.SemaphoreType.DMA((2, 7)),
        pltpu.SemaphoreType.DMA((2, 7)),
        pltpu.SemaphoreType.DMA((4,)),
    ]
    return pl.pallas_call(
        kernel,
        out_shape=jax.ShapeDtypeStruct(shape, jnp.float32),
        in_specs=[pl.BlockSpec(memory_space=pltpu.HBM)] * 2,
        out_specs=pl.BlockSpec(memory_space=pltpu.VMEM),
        scratch_shapes=scratch,
        compiler_params=pltpu.CompilerParams(
            collective_id=0, has_side_effects=True, vmem_limit_bytes=24 * 1024 * 1024),
        name="sweeps",
    )


def solution(mesh):
    sizes = mesh.shape

    def on_device(source_field, labels):
        return make_kernel(sizes["phi"], sizes["row"], sizes["gz"], labels.shape)(source_field, labels)

    placed = (P(None, ("group", "phi"), "gz", "row"), P(("group", "phi"), "gz", "row"))
    return jax.shard_map(
        on_device,
        mesh=mesh,
        in_specs=placed,
        out_specs=P(("group", "phi"), "gz", "row"),
        check_vma=False,
    )
```

```python
import jax
import jax.numpy as jnp
from jax import lax
from jax.experimental import pallas as pl
from jax.experimental.pallas import tpu as pltpu
from jax.sharding import PartitionSpec as P

ITERS = 4
iron_perm = 40.0
iron_sat = 0.25
coil_perm = 4.0
coil_sat = 1.0
step_cap = 0.1
spectral = 0.9
MESH = pl.DeviceIdType.MESH


def chebyshev_weights(sweep_count):
    weights = [1.0]
    weights.append(1.0 / (1.0 - spectral * spectral / 2.0))
    while len(weights) < sweep_count:
        weights.append(1.0 / (1.0 - spectral * spectral * weights[-1] / 4.0))
    return weights


def make_kernel(n_phi, n_row, n_gz, shape):
    s_phi, s_z, s_r = shape
    peers = n_phi * n_row * n_gz
    half = s_phi // 2
    wide = 2 * s_r
    tall = s_z + 8
    cell_count = s_phi * s_z * s_r * peers
    weights = chebyshev_weights(ITERS)
    first, last = 2, half + 1

    def kernel(src, lab, out, S, L, A, B, Pot, M, U, G, FP, FU, X, XL, sum_sem, halo_send, halo_recv, in_send, in_recv, loc_sem):
        p = lax.axis_index("phi")
        c = lax.axis_index("row")
        g = lax.axis_index("gz")
        lanes = pl.ds(pl.multiple_of(c * s_r, s_r), s_r)
        sib = 1 - c

        def own_part(core):
            return pl.ds((half - 1) * core, half + 1), pl.ds(2 - core, half + 1)

        def cut(ref, rows, z):
            return ref.at[:, rows, z, :] if ref is src or ref is X else ref.at[rows, z, :]

        def land(ref, rows, z):
            return ref.at[:, rows, z, lanes] if ref is S else ref.at[rows, z, lanes]

        whole_z = pl.ds(0, s_z)
        local, stages = [], []
        for n, (a, b, staged) in enumerate(((src, S, X), (lab, L, XL))):
            stage = pltpu.make_async_copy(a, staged, loc_sem.at[2 + n])
            stage.start()
            stages.append(stage)
            frm, to = own_part(c)
            copy = pltpu.make_async_copy(cut(a, frm, whole_z), land(b, to, whole_z), loc_sem.at[n])
            copy.start()
            local.append(copy)

        def along_phi(d):
            if n_phi == 4 and peers <= 32:
                return (p, p + 1 - 2 * lax.rem(p, 2), lax.rem(p + 2, 4), 3 - p)[d]
            return lax.rem(p + d, n_phi)

        def peer(j):
            return {
                "phi": along_phi(j // (n_row * n_gz)),
                "row": lax.rem(c + (j // n_gz) % n_row, n_row),
                "gz": lax.rem(g + j % n_gz, n_gz),
            }

        def each_peer(body):
            if peers > 32:
                lax.fori_loop(1, peers, lambda j, carry: (body(j, peer(j)), carry)[1], 0)
            else:
                for j, where in peer_list:
                    body(j, where)

        if peers <= 32:
            per_chip = n_row * n_gz
            order = sorted(range(1, peers), key=lambda j: (-(j // per_chip), -(j % n_gz)))
            peer_list = [(j, peer(j)) for j in order]

        rim = pl.ds(s_z, 8)
        S[:, :, rim, :] = jnp.zeros((3, half + 4, 8, wide), jnp.float32)
        L[:, rim, :] = jnp.zeros((half + 4, 8, wide), jnp.int32)
        for k in range(ITERS - 1):
            U[k, :, rim, :] = jnp.zeros((half + 4, 8, wide), jnp.float32)

        barrier = pltpu.get_barrier_semaphore()

        def greet(j, where):
            pl.semaphore_signal(barrier, inc=1, device_id=where, device_id_type=MESH)

        each_peer(greet)
        pl.semaphore_wait(barrier, peers - 1)

        for stage in stages:
            stage.wait()
        up_p, down_p = lax.rem(p + 1, n_phi), lax.rem(p + n_phi - 1, n_phi)
        has_up, has_down = g < n_gz - 1, g > 0
        up_g, down_g = jnp.minimum(g + 1, n_gz - 1), jnp.maximum(g - 1, 0)

        always, when_up, when_down = [], [], []
        for n, (a, b) in enumerate(((X, S), (XL, L))):
            def remote(frm, to, send, recv, where, n=n):
                return pltpu.make_async_remote_copy(
                    src_ref=frm, dst_ref=to, send_sem=in_send.at[n, send], recv_sem=in_recv.at[n, recv],
                    device_id=where, device_id_type=MESH)

            frm, to = own_part(sib)
            always.append(remote(cut(a, pl.ds(s_phi - 1, 1), whole_z), land(b, pl.ds(1, 1), whole_z), 1, 1 + c,
                                 {"phi": up_p, "row": 0}))
            always.append(remote(cut(a, pl.ds(0, 1), whole_z), land(b, pl.ds(last + 1, 1), whole_z), 2, 1 + c,
                                 {"phi": down_p, "row": 1}))
            always.append(remote(cut(a, frm, whole_z), land(b, to, whole_z), 0, 0, {"row": sib}))
            for t in range(2):
                rows = pl.ds(half * t, half)
                when_up.append(remote(cut(a, rows, pl.ds(s_z - 1, 1)), land(b, pl.ds(first, half), pl.ds(tall - 1, 1)),
                                      3 + t, 3 + c, {"gz": up_g, "row": t}))
                when_down.append(remote(cut(a, rows, pl.ds(0, 1)), land(b, pl.ds(first, half), pl.ds(s_z, 1)),
                                        5 + t, 5 + c, {"gz": down_g, "row": t}))

        def start_all(copies):
            for copy in copies:
                copy.start()

        def send_wait_all(copies):
            for copy in copies:
                copy.wait_send()

        start_all(always)

        @pl.when(has_up)
        def _():
            start_all(when_up)

        @pl.when(has_down)
        def _():
            start_all(when_down)

        def arrived(b, n, slot, rows, z, ln):
            ref = b.at[:, rows, z, ln] if b is S else b.at[rows, z, ln]
            pltpu.make_async_remote_copy(
                src_ref=ref, dst_ref=ref, send_sem=in_send.at[n, 0], recv_sem=in_recv.at[n, slot],
                device_id={"row": sib}, device_id_type=MESH).wait_recv()

        def first_perm(i, z):
            label = L[i, z]
            a = jnp.where(label == 1, iron_perm - 1.0, jnp.where(label == 2, coil_perm - 1.0, 0.0))
            b = jnp.where(label == 1, 1.0 / iron_sat, jnp.where(label == 2, 1.0 / coil_sat, 0.0))
            A[i, z] = a
            B[i, z] = b
            s0, s1, s2 = S[0, i, z], S[1, i, z], S[2, i, z]
            M[i, z] = 1.0 + a / (1.0 + (s0 * s0 + s1 * s1 + s2 * s2) * b)

        for copy in local:
            copy.wait()
        for n, b in enumerate((S, L)):
            arrived(b, n, 0, own_part(c)[1], whole_z, pl.ds(pl.multiple_of(sib * s_r, s_r), s_r))
        for i in range(first, last + 1):
            first_perm(i, whole_z)
        near = jnp.where(c == 0, last + 1, 1)
        first_perm(near, whole_z)
        for n, b in enumerate((S, L)):
            for core in range(2):
                arrived(b, n, 1 + core, pl.ds(jnp.where(c == 0, 1, last + 1), 1), whole_z, pl.ds(core * s_r, s_r))
        first_perm(last + 2 - near, whole_z)

        @pl.when(has_down)
        def _():
            for n, b in enumerate((S, L)):
                for core in range(2):
                    arrived(b, n, 3 + core, pl.ds(first, half), pl.ds(tall - 1, 1), pl.ds(core * s_r, s_r))

        @pl.when(has_up)
        def _():
            for n, b in enumerate((S, L)):
                for core in range(2):
                    arrived(b, n, 5 + core, pl.ds(first, half), pl.ds(s_z, 1), pl.ds(core * s_r, s_r))

        for i in range(1, last + 2):
            first_perm(i, rim)

        lane = lax.broadcasted_iota(jnp.int32, (tall, wide), 1)
        at_end, at_start = lane == wide - 1, lane == 0

        def z_up(x):
            return pltpu.roll(x, tall - 1, 0)

        def z_down(x):
            return pltpu.roll(x, 1, 0)

        def r_up(x, edge):
            return jnp.where(at_end[: x.shape[0]], edge, pltpu.roll(x, wide - 1, 1))

        def r_down(x, edge):
            return jnp.where(at_start[: x.shape[0]], edge, pltpu.roll(x, 1, 1))

        def conduct(a, b):
            return 2.0 * a * b / (a + b)

        q_up = {"phi": jnp.where(c == 1, up_p, p), "row": sib}
        q_down = {"phi": jnp.where(c == 0, down_p, p), "row": sib}
        z_top, z_low = pl.ds(s_z - 2, 2), pl.ds(0, 2)
        at_low, at_top = pl.ds(tall - 2, 2), pl.ds(s_z, 2)

        def halo(k, slot):
            def ref(rows, z):
                return U.at[k, rows, z, :]

            own = pl.ds(first, half)
            frm, to, where = (
                (ref(pl.ds(last - 1, 2), whole_z), ref(pl.ds(0, 2), whole_z), q_up),
                (ref(pl.ds(first, 2), whole_z), ref(pl.ds(last + 1, 2), whole_z), q_down),
                (ref(own, z_top), ref(own, at_low), {"gz": up_g}),
                (ref(own, z_low), ref(own, at_top), {"gz": down_g}),
                (ref(pl.ds(last, 1), z_top), ref(pl.ds(1, 1), at_low), dict(q_up, gz=up_g)),
                (ref(pl.ds(first, 1), z_top), ref(pl.ds(last + 1, 1), at_low), dict(q_down, gz=up_g)),
                (ref(pl.ds(last, 1), z_low), ref(pl.ds(1, 1), at_top), dict(q_up, gz=down_g)),
                (ref(pl.ds(first, 1), z_low), ref(pl.ds(last + 1, 1), at_top), dict(q_down, gz=down_g)),
            )[slot]
            return pltpu.make_async_remote_copy(
                src_ref=frm, dst_ref=to, send_sem=halo_send.at[k, slot], recv_sem=halo_recv.at[k, slot],
                device_id=where, device_id_type=MESH)

        UP, DOWN, BOTH = (2, 4, 5), (3, 6, 7), (0, 1)

        def halo_start(k):
            start_all([halo(k, s) for s in BOTH])

            @pl.when(has_up)
            def _():
                start_all([halo(k, s) for s in UP])

            @pl.when(has_down)
            def _():
                start_all([halo(k, s) for s in DOWN])

        def halo_arrive(k):
            for s in BOTH:
                halo(k, s).wait_recv()

            @pl.when(has_down)
            def _():
                for s in UP:
                    halo(k, s).wait_recv()

            @pl.when(has_up)
            def _():
                for s in DOWN:
                    halo(k, s).wait_recv()

        def halo_sent(k):
            send_wait_all([halo(k, s) for s in BOTH])

            @pl.when(has_up)
            def _():
                send_wait_all([halo(k, s) for s in UP])

            @pl.when(has_down)
            def _():
                send_wait_all([halo(k, s) for s in DOWN])

        def swap(frm, to, slot):
            return pltpu.make_async_remote_copy(
                src_ref=frm, dst_ref=to, send_sem=halo_send.at[ITERS - 1, slot], recv_sem=halo_recv.at[ITERS - 1, slot],
                device_id={"row": sib}, device_id_type=MESH)

        other_lanes = pl.ds(pl.multiple_of(sib * s_r, s_r), s_r)
        own_rows = pl.ds(first, half)

        def total_wait(k):
            return pltpu.make_async_remote_copy(
                src_ref=G.at[k, pl.ds(1, peers - 1)], dst_ref=G.at[k, pl.ds(1, peers - 1)],
                send_sem=sum_sem.at[0, k], recv_sem=sum_sem.at[1, k], device_id={"row": sib}, device_id_type=MESH)

        for k in range(ITERS):
            cur = k % 2

            def fresh(i, k=k, cur=cur):
                new = wide_factor * U[k - 1, i]
                if k > 1:
                    new = new + Pot[1 - cur, i]
                Pot[cur, i] = new
                return new

            def perm_row(i, carry, k=k, cur=cur):
                before, here = carry
                after = fresh(i + 1)
                s0 = S[0, i] - 0.5 * (after - before)
                s1 = S[1, i] - 0.5 * (z_up(here) - z_down(here))
                s2 = S[2, i] - 0.5 * (r_up(here, 0.0) - r_down(here, 0.0))
                field_sq = s0 * s0 + s1 * s1 + s2 * s2
                M[i] = 1.0 + A[i] / (1.0 + field_sq * B[i])
                return here, after

            if k > 0:
                lax.fori_loop(1, half + 3, perm_row, (fresh(0), fresh(1)), unroll=True)
                if k == ITERS - 1:
                    give_potential = swap(Pot.at[cur, own_rows, whole_z, other_lanes], FP, 0)
                    give_potential.start()

            def relax_row(i, carry, k=k, cur=cur):
                below, acc = carry
                m = M[i]
                mi = m[:s_z]
                above = conduct(mi, M[i + 1, :s_z])
                cz = conduct(m, z_up(m))
                cz_low = z_down(cz)[:s_z]
                cz = cz[:s_z]
                cr = conduct(mi, r_up(mi, 1.0))
                cr_low = jnp.where(at_start[:s_z], 2.0 * mi / (mi + 1.0), pltpu.roll(cr, 1, 1))
                fz = m * S[1, i]
                fr = mi * S[2, i, :s_z]
                flux = M[i + 1, :s_z] * S[0, i + 1, :s_z] - M[i - 1, :s_z] * S[0, i - 1, :s_z]
                flux = flux + (z_up(fz) - z_down(fz))[:s_z] + (r_up(fr, 0.0) - r_down(fr, 0.0))
                numerator = -0.5 * flux
                if k > 0:
                    here = Pot[cur, i]
                    hi = here[:s_z]
                    numerator = (numerator + above * Pot[cur, i + 1, :s_z] + below * Pot[cur, i - 1, :s_z]
                                 + cz * z_up(here)[:s_z] + cz_low * z_down(here)[:s_z]
                                 + cr * r_up(hi, 0.0) + cr_low * r_down(hi, 0.0))
                relaxed = numerator / (above + below + cz + cz_low + cr + cr_low)
                if k == 0:
                    update = weights[0] * relaxed
                elif k == 1:
                    update = weights[1] * relaxed - hi
                else:
                    earlier = Pot[1 - cur, i, :s_z]
                    update = earlier + weights[k] * (relaxed - earlier) - hi
                U[k, i, :s_z] = update
                return above, acc + update * update

            start = conduct(M[1, :s_z], M[2, :s_z])
            _, acc = lax.fori_loop(first, last + 1, relax_row, (start, jnp.zeros((s_z, wide), jnp.float32)), unroll=True)

            acc = acc[:, :s_r] + acc[:, s_r:]
            part = acc[:8]
            for z in range(8, s_z, 8):
                part = part + acc[z : z + 8]
            G[k, 0:1] = jnp.sum(part, axis=0, keepdims=True)

            def share(j, where, k=k):
                pltpu.make_async_remote_copy(
                    src_ref=G.at[k, pl.ds(0, 1)], dst_ref=G.at[k, pl.ds(j, 1)], send_sem=sum_sem.at[0, k],
                    recv_sem=sum_sem.at[1, k], device_id=where, device_id_type=MESH).start()

            each_peer(share)
            if k < ITERS - 1:
                halo_start(k)
            else:
                give_update = swap(U.at[k, own_rows, whole_z, other_lanes], FU, 1)
                give_update.start()
            total_wait(k).wait_recv()
            sum_squares = jnp.sum(jnp.sum(G[k], axis=0, keepdims=True), axis=1, keepdims=True)
            factor = jnp.minimum(1.0, step_cap * lax.rsqrt(sum_squares * (1.0 / cell_count) + 1e-06))

            if k < ITERS - 1:
                halo_arrive(k)
                wide_factor = jnp.broadcast_to(factor, (tall, wide))

            else:
                wide_factor = jnp.broadcast_to(factor, (half, s_z, s_r))
                out[pl.ds(half * c, half)] = (
                    Pot[cur, first : last + 1, :s_z, lanes] + wide_factor * U[k, first : last + 1, :s_z, lanes])
                give_potential.wait_recv()
                give_update.wait_recv()
                out[pl.ds(half * sib, half)] = FP[...] + wide_factor * FU[...]

        send_wait_all(always)

        @pl.when(has_up)
        def _():
            send_wait_all(when_up)

        @pl.when(has_down)
        def _():
            send_wait_all(when_down)

        for k in range(ITERS):
            total_wait(k).wait_send()
            if k < ITERS - 1:
                halo_sent(k)
        give_potential.wait_send()
        give_update.wait_send()

    rows = half + 4
    scratch = [
        pltpu.VMEM((3, rows, tall, wide), jnp.float32),
        pltpu.VMEM((rows, tall, wide), jnp.int32),
        pltpu.VMEM((rows, tall, wide), jnp.float32),
        pltpu.VMEM((rows, tall, wide), jnp.float32),
        pltpu.VMEM((2, rows, tall, wide), jnp.float32),
        pltpu.VMEM((rows, tall, wide), jnp.float32),
        pltpu.VMEM((ITERS, rows, tall, wide), jnp.float32),
        pltpu.VMEM((ITERS, peers, s_r), jnp.float32),
        pltpu.VMEM((half, s_z, s_r), jnp.float32),
        pltpu.VMEM((half, s_z, s_r), jnp.float32),
        pltpu.VMEM((3,) + tuple(shape), jnp.float32),
        pltpu.VMEM(tuple(shape), jnp.int32),
        pltpu.SemaphoreType.DMA((2, ITERS)),
        pltpu.SemaphoreType.DMA((ITERS, 8)),
        pltpu.SemaphoreType.DMA((ITERS, 8)),
        pltpu.SemaphoreType.DMA((2, 7)),
        pltpu.SemaphoreType.DMA((2, 7)),
        pltpu.SemaphoreType.DMA((4,)),
    ]
    return pl.pallas_call(
        kernel,
        out_shape=jax.ShapeDtypeStruct(shape, jnp.float32),
        in_specs=[pl.BlockSpec(memory_space=pltpu.HBM)] * 2,
        out_specs=pl.BlockSpec(memory_space=pltpu.VMEM),
        scratch_shapes=scratch,
        compiler_params=pltpu.CompilerParams(
            collective_id=0, has_side_effects=True, vmem_limit_bytes=24 * 1024 * 1024),
        name="sweeps",
    )


def solution(mesh):
    sizes = mesh.shape

    def on_device(source_field, labels):
        return make_kernel(sizes["phi"], sizes["row"], sizes["gz"], labels.shape)(source_field, labels)

    placed = (P(None, ("group", "phi"), "gz", "row"), P(("group", "phi"), "gz", "row"))
    return jax.shard_map(
        on_device,
        mesh=mesh,
        in_specs=placed,
        out_specs=P(("group", "phi"), "gz", "row"),
        check_vma=False,
    )
```
